32 devices in a mesh: batch: 8 (over y, x, core), head: 4 (over z).
Axes of the slice: x: 2, y: 2, z: 4, core: 2. Of those that a mesh axis runs over, the one named last changes fastest.
Arguments:
- inputs: bfloat16 [8192, 1024], P('batch'), may hold values from -6 to 6
- segment_ids: int32 [8192], P('batch'), may hold values from 0 to 63, never falling along the last dimension, each value on 1 to 512 neighbouring positions
- query_weight: bfloat16 [1024, 1024], P(None, 'head'), may hold values from -0.1875 to 0.1875
- query_bias: float32 [1024], P('head'), may hold values from -3 to 3
- key_weight: bfloat16 [1024, 1024], P(None, 'head'), may hold values from -0.1875 to 0.1875
- value_weight: bfloat16 [1024, 1024], P(None, 'head'), may hold values from -0.1875 to 0.1875
- value_bias: float32 [1024], P('head'), may hold values from -3 to 3
- output_weight: bfloat16 [1024, 1024], P('head'), may hold values from -0.75 to 0.75
- output_bias: float32 [1024], replicated, may hold values from -3 to 3
- attn_gain: float32 [1024], replicated, may hold values from 0.5 to 1.5
- attn_shift: float32 [1024], replicated, may hold values from -2 to 2
- up_weight: bfloat16 [1024, 4096], P(None, 'head'), may hold values from -0.1875 to 0.1875
- up_bias: float32 [4096], P('head'), may hold values from -3 to 3
- down_weight: bfloat16 [4096, 1024], P('head'), may hold values from -0.09375 to 0.09375
- down_bias: float32 [1024], replicated, may hold values from -3 to 3
- ffn_gain: float32 [1024], replicated, may hold values from 0.5 to 1.5
- ffn_shift: float32 [1024], replicated, may hold values from -2 to 2
- lexical_weight: float32 [1024], replicated, may hold values from -0.1875 to 0.1875
- out_cotangent: bfloat16 [8192, 1024], P(('batch', 'head')), may hold values from -6 to 6
- lexical_cotangent: bfloat16 [8192], P(('batch', 'head')), may hold values from -6 to 6
Outputs:
- result: bfloat16 [8192, 1024], P(('batch', 'head'))
- lexical: float32 [8192], P(('batch', 'head'))
- grad_inputs: bfloat16 [8192, 1024], P(('batch', 'head'))
- grad_query_weight: float32 [1024, 1024], P(None, 'head')
- grad_query_bias: float32 [1024], P('head')
- grad_key_weight: float32 [1024, 1024], P(None, 'head')
- grad_value_weight: float32 [1024, 1024], P(None, 'head')
- grad_value_bias: float32 [1024], P('head')
- grad_output_weight: float32 [1024, 1024], P('head')
- grad_output_bias: float32 [1024], replicated
- grad_attn_gain: float32 [1024], replicated
- grad_attn_shift: float32 [1024], replicated
- grad_up_weight: float32 [1024, 4096], P(None, 'head')
- grad_up_bias: float32 [4096], P('head')
- grad_down_weight: float32 [4096, 1024], P('head')
- grad_down_bias: float32 [1024], replicated
- grad_ffn_gain: float32 [1024], replicated
- grad_ffn_shift: float32 [1024], replicated
- grad_lexical_weight: float32 [1024], replicated
- mean_lexical: float32 [], replicated
- active_share: float32 [], replicated
The draws below stay inside these ranges and needn't reach their ends.
Inputs may be any that keep to these rules, and one draw needn't show every extreme that they name: segment_ids never fall along the tokens, each text has 1 to 512 tokens and one has exactly 512; a text cut by the end of a row counts as two texts.
All inputs are finite; a program needn't handle non-finite values.
Results may differ from the reference program's by a relative error of at most 0.033.
Values may be sent and summed in bfloat16 or wider, within the bound.
No kernel may reach another device: no remote copies, remote signals or barrier semaphores. Data moves between devices by JAX's collectives and lax.ppermute only.
A program may use at most 192 MiB of HBM per device.

```python
import math
import jax
import jax.numpy as jnp
import numpy as np
from jax import lax

D = 1024
HEADS = 16
HEAD_DIM = 64
FF = 4096
ROW_LEN = 1024
TOKENS = 8192
TEXTS = 8
MOST = 512
N_BATCH = 8
N_HEAD = 4


def shard_levels(key, shape, pieces, smallest, largest):
    def one(position, shards_of):
        steps = jax.random.uniform(jax.random.fold_in(jax.random.fold_in(key, 6), position), (shards_of,), jnp.float32, smallest / len(pieces), largest / len(pieces))
        return jnp.repeat(jnp.exp(steps), shape[position] // shards_of).reshape((-1,) + (1,) * (len(shape) - position - 1))

    loudness = one(*pieces[0])
    for cut in pieces[1:]:
        loudness = loudness * one(*cut)
    return loudness


def length_profile(count, total, most, skew):
    weights = [(1 << 20) // math.isqrt(standing ** skew) + 1 for standing in range(2, count + 1)]
    spare, holding = total - most - (count - 1), [1] * (count - 1)
    while spare > 0:
        candidates = [i for i in range(count - 1) if holding[i] < most]
        whole, budget = sum([weights[i] for i in candidates]), spare
        for i in candidates:
            more = min(most - holding[i], max(1, budget * weights[i] // whole), spare)
            holding[i] = holding[i] + more
            spare = spare - more
    return np.array([most] + holding)


def uneven_parts(key, count, total, bound, lean):
    if count == 2:
        one = jax.random.randint(key, (), max(1, total - bound), min(bound, total - 1) + 1)
        return jnp.stack([one, total - one])
    tallies = jnp.asarray(length_profile(count, total, bound, lean), jnp.int32)
    couples = (count - 1) // 2
    giver, taker = tallies[1:1 + 2 * couples:2], tallies[2:2 + 2 * couples:2]
    slack = jnp.minimum(giver - 1, bound - taker)
    shifted = jax.random.randint(jax.random.fold_in(key, 1), (couples,), 0, 1 << 20) % (slack + 1)
    tallies = tallies.at[1:1 + 2 * couples:2].set(giver - shifted).at[2:2 + 2 * couples:2].set(taker + shifted)
    return tallies[jax.random.permutation(jax.random.fold_in(key, 2), count)]


def bell_draw(key, dims, deviation, most, shards=(), held_as=jnp.bfloat16):
    values = jax.random.normal(key, dims, jnp.float32) * deviation
    if len(shards) > 0:
        values = shard_levels(key, dims, shards, -0.22, 0.18) * values
    return jnp.clip(values, min=-most, max=most).astype(held_as)


def setup_inputs(seed: int = 0) -> dict:
    keys = jax.random.split(jax.random.key(seed), 21)
    inputs = bell_draw(keys[0], (TOKENS, D), 1.0, 6.0, ((0, 8),))
    segment_ids = jnp.searchsorted(jnp.cumsum(uneven_parts(keys[1], TEXTS * N_BATCH, TOKENS, MOST, 2)), jnp.arange(TOKENS), side="right").astype(jnp.int32)
    query_weight = bell_draw(keys[2], (D, D), D ** -0.5, 0.1875, ((1, 4),))
    query_bias = bell_draw(keys[3], (D,), 0.5, 3.0, ((0, 4),), jnp.float32)
    key_weight = bell_draw(keys[4], (D, D), D ** -0.5, 0.1875, ((1, 4),))
    value_weight = bell_draw(keys[5], (D, D), D ** -0.5, 0.1875, ((1, 4),))
    value_bias = bell_draw(keys[6], (D,), 0.5, 3.0, ((0, 4),), jnp.float32)
    output_weight = bell_draw(keys[7], (D, D), (D // 16) ** -0.5, 0.75, ((0, 4),))
    output_bias = bell_draw(keys[8], (D,), 0.5, 3.0, (), jnp.float32)
    attn_gain = jnp.clip(1.0 + 0.1 * jax.random.normal(keys[9], (D,), jnp.float32), 0.5, 1.5)
    attn_shift = bell_draw(keys[10], (D,), 0.3, 2.0, (), jnp.float32)
    up_weight = bell_draw(keys[11], (D, FF), D ** -0.5, 0.1875, ((1, 4),))
    up_bias = bell_draw(keys[12], (FF,), 0.5, 3.0, ((0, 4),), jnp.float32)
    down_weight = bell_draw(keys[13], (FF, D), FF ** -0.5, 0.09375, ((0, 4),))
    down_bias = bell_draw(keys[14], (D,), 0.5, 3.0, (), jnp.float32)
    ffn_gain = jnp.clip(1.0 + 0.1 * jax.random.normal(keys[15], (D,), jnp.float32), 0.5, 1.5)
    ffn_shift = bell_draw(keys[16], (D,), 0.3, 2.0, (), jnp.float32)
    lexical_weight = bell_draw(keys[17], (D,), D ** -0.5, 0.1875, (), jnp.float32)
    out_cotangent = bell_draw(keys[18], (TOKENS, D), 1.0, 6.0, ((0, 32),))
    lexical_cotangent = bell_draw(keys[19], (TOKENS,), 1.0, 6.0, ((0, 32),))
    return {"inputs": inputs, "segment_ids": segment_ids, "query_weight": query_weight, "query_bias": query_bias, "key_weight": key_weight, "value_weight": value_weight, "value_bias": value_bias, "output_weight": output_weight, "output_bias": output_bias, "attn_gain": attn_gain, "attn_shift": attn_shift, "up_weight": up_weight, "up_bias": up_bias, "down_weight": down_weight, "down_bias": down_bias, "ffn_gain": ffn_gain, "ffn_shift": ffn_shift, "lexical_weight": lexical_weight, "out_cotangent": out_cotangent, "lexical_cotangent": lexical_cotangent}


norm_eps = 1e-05
highest = lax.Precision.HIGHEST

@jax.custom_vjp
def low(v):
    return lax.optimization_barrier(v.astype(jnp.bfloat16)).astype(jnp.float32)

@jax.custom_vjp
def low_back(v):
    return v

def low_keep(v):
    return (low(v), None)

def low_pass(kept, grad):
    return (grad,)

def back_keep(v):
    return (v, None)

def back_low(kept, grad):
    return (low(grad),)
low.defvjp(low_keep, low_pass)
low_back.defvjp(back_keep, back_low)

def layer_norm(value, gain, shift):
    center = value - lax.optimization_barrier(jnp.mean(value, -1, keepdims=True))
    spread = lax.optimization_barrier(jnp.mean(center * center, -1, keepdims=True))
    return center * lax.rsqrt(spread + norm_eps) * gain + shift

def block_rows(length):
    return length // 4 if length >= 2048 else length

def attend(queries, key_rows, value_rows, seg_row):
    length = queries.shape[0]
    block_len = block_rows(length)
    block_count = length // block_len
    query_blocks = queries.reshape(block_count, block_len, HEADS, HEAD_DIM)
    seg_blocks = seg_row.reshape(block_count, block_len)

    def forward_block(block_item):
        query_part, seg_part = block_item
        scores = jnp.einsum('qhe,khe->hqk', query_part, key_rows, precision=highest)
        scores = low_back(scores)
        same_text = (seg_part[:, None] == seg_row[None, :])[None]
        scores = jnp.where(same_text, scores, -1000000000.0)
        row_max = lax.optimization_barrier(jnp.max(scores, -1, keepdims=True))
        exp_terms = jnp.exp(scores - row_max)
        attn_prob = low(exp_terms / lax.optimization_barrier(jnp.sum(exp_terms, -1, keepdims=True)))
        return jnp.einsum('hqk,khe->qhe', attn_prob, value_rows, precision=highest)
    attended = lax.map(jax.checkpoint(forward_block), (query_blocks, seg_blocks))
    return attended.reshape(length, HEADS * HEAD_DIM)

def group_sum(left_rows, right_mat):
    group_width = left_rows.shape[1] // N_HEAD
    left_grp = left_rows.reshape(left_rows.shape[0], N_HEAD, group_width)
    right_grp = right_mat.reshape(N_HEAD, group_width, right_mat.shape[1])
    partials = low(jnp.einsum('lgc,gcd->gld', left_grp, right_grp, precision=highest))
    return low_back(lax.optimization_barrier(jnp.sum(partials, 0)))

def forward(params, row_in, seg_row):
    query_w, query_b, key_w, value_w, value_b, out_w, out_b, gain_one, shift_one, up_w, up_b, down_w, down_b, gain_two, shift_two, lex_w = params
    queries = low(low_back((jnp.dot(row_in, query_w, precision=highest) + query_b) * 0.125))
    key_rows = low(low_back(jnp.dot(row_in, key_w, precision=highest)))
    value_rows = low(low_back(jnp.dot(row_in, value_w, precision=highest) + value_b))
    length = row_in.shape[0]
    shape_three = (length, HEADS, HEAD_DIM)
    mixed_rows = low(low_back(attend(queries.reshape(shape_three), key_rows.reshape(shape_three), value_rows.reshape(shape_three), seg_row)))
    normed = layer_norm(row_in + group_sum(mixed_rows, out_w) + out_b, gain_one, shift_one)
    hidden = low_back(jnp.dot(low(normed), up_w, precision=highest) + up_b)
    active = low(jax.nn.gelu(hidden, approximate=False))
    final = layer_norm(normed + group_sum(active, down_w) + down_b, gain_two, shift_two)
    lexical = jax.nn.softplus(jnp.dot(final, lex_w, precision=highest))
    return (final, lexical)

def reference(inputs, segment_ids, query_weight, query_bias, key_weight, value_weight, value_bias, output_weight, output_bias, attn_gain, attn_shift, up_weight, up_bias, down_weight, down_bias, ffn_gain, ffn_shift, lexical_weight, out_cotangent, lexical_cotangent):
    params = tuple((item.astype(jnp.float32) for item in (query_weight, query_bias, key_weight, value_weight, value_bias, output_weight, output_bias, attn_gain, attn_shift, up_weight, up_bias, down_weight, down_bias, ffn_gain, ffn_shift, lexical_weight)))
    rows_in = inputs.astype(jnp.float32).reshape(N_BATCH, ROW_LEN, D)
    seg_rows = segment_ids.reshape(N_BATCH, ROW_LEN)
    cot_rows = out_cotangent.astype(jnp.float32).reshape(N_BATCH, ROW_LEN, D)
    lex_cots = lexical_cotangent.astype(jnp.float32).reshape(N_BATCH, ROW_LEN)

    def step(totals, row_item):
        row_in, seg_row, cot_row, lex_cot = row_item
        outputs, pull = jax.vjp(lambda p, v: forward(p, v, seg_row), params, row_in)
        grad_params, grad_row = pull((cot_row, lex_cot))
        totals = jax.tree.map(lambda a, b: a + b, totals, grad_params)
        return (totals, (outputs[0].astype(jnp.bfloat16), outputs[1], grad_row.astype(jnp.bfloat16)))
    zeros = jax.tree.map(jnp.zeros_like, params)
    grads, (results, lexicals, grad_rows) = lax.scan(step, zeros, (rows_in, seg_rows, cot_rows, lex_cots))
    later = jnp.concatenate([jnp.zeros((N_BATCH, 1), jnp.float32), (seg_rows[:, 1:] == seg_rows[:, :-1]).astype(jnp.float32)], 1)
    later_count = jnp.sum(later)
    mean_lexical = jnp.sum(lexicals * later) / later_count
    active_share = later_count / (N_BATCH * ROW_LEN)
    return (results.reshape(N_BATCH * ROW_LEN, D), lexicals.reshape(N_BATCH * ROW_LEN), grad_rows.reshape(N_BATCH * ROW_LEN, D), grads[0], grads[1], grads[2], grads[3], grads[4], grads[5], grads[6], grads[7], grads[8], grads[9], grads[10], grads[11], grads[12], grads[13], grads[14], grads[15], mean_lexical, active_share)
```

```python
import functools
import math

import jax
import jax.numpy as jnp
from jax import lax
from jax.experimental import pallas as pl
from jax.experimental.pallas import tpu as pltpu
from jax.sharding import Mesh, PartitionSpec as P

HEAD_DIM = 64
LANES = 128
TILE = 256
SMALL = 16
NORM_EPS = 1e-05
MASKED = -1000000000.0
ALL = ("p", "c", "g", "l")
PLANE = ("p", "c")
LINE = ("g", "l")
f32 = jnp.float32
bf16 = jnp.bfloat16
MIB = 2**20
VMEM = pl.BlockSpec(memory_space=pltpu.VMEM)
SMEM = pl.BlockSpec(memory_space=pltpu.SMEM)
HBM = pl.BlockSpec(memory_space=pltpu.HBM)


def shape(dims, dtype):
    return jax.ShapeDtypeStruct(dims, dtype)


def nn(left, right):
    return jnp.dot(left, right, preferred_element_type=f32)


def nt(left, right):
    return lax.dot_general(left, right, (((1,), (1,)), ((), ())), preferred_element_type=f32)


def tn(left, right):
    return lax.dot_general(left, right, (((0,), (0,)), ((), ())), preferred_element_type=f32)


def call(kernel, name, out_shape, args, scalars=0, scratch=(), us=1.0, vmem=12, far=False, cols=None):
    many = isinstance(out_shape, (list, tuple))
    outs = list(out_shape) if many else [out_shape]
    n_in, n_out = len(args), len(outs)
    far_in = range(scalars, n_in) if far else ()
    far_out = range(n_out) if far else ()
    cols = cols or {}
    held = [pltpu.VMEM(args[i].shape[:-1] + ((LANES,) if i in cols else args[i].shape[-1:]), args[i].dtype) for i in far_in]
    held += [pltpu.VMEM(outs[i].shape, outs[i].dtype) for i in far_out]
    n_held = len(held)

    def whole(*refs):
        given, extra = refs[: n_in + n_out], refs[n_in + n_out :]
        use = list(given)
        own, rest = extra[:n_held], extra[n_held:]
        if n_held:
            rest, sems = rest[:-1], rest[-1]
        copies = []
        for slot, i in enumerate(far_in):
            source = given[i]
            if i in cols:
                source = source.at[:, cols[i]]
            copies.append(pltpu.make_async_copy(source, own[slot], sems.at[slot]))
            use[i] = own[slot]
        for copy in copies:
            copy.start()
        for copy in copies:
            copy.wait()
        for slot, i in enumerate(far_out, len(far_in)):
            use[n_in + i] = own[slot]
        kernel(*use, *rest)
        copies = [
            pltpu.make_async_copy(own[slot], given[n_in + i], sems.at[slot]) for slot, i in enumerate(far_out, len(far_in))
        ]
        for copy in copies:
            copy.start()
        for copy in copies:
            copy.wait()

    place = HBM if far else VMEM
    result = pl.pallas_call(
        whole if n_held else kernel,
        out_shape=outs,
        in_specs=[SMEM] * scalars + [place] * (n_in - scalars),
        out_specs=[place] * n_out,
        scratch_shapes=held + list(scratch) + ([pltpu.SemaphoreType.DMA((n_held,))] if n_held else []),
        compiler_params=pltpu.CompilerParams(vmem_limit_bytes=(58 if far else vmem) * MIB),
        cost_estimate=pl.CostEstimate(flops=int(us * 1.1e7), bytes_accessed=int(us * 3.6e4), transcendentals=0),
        name=name,
    )(*args)
    return list(result) if many else result[0]


def rows_at(index, count):
    return pl.ds(pl.multiple_of(index * count, count), count)


def seg_columns(seg_ref, col_ref):
    seg = seg_ref[...].astype(f32)
    col_ref[...] = jnp.transpose(jnp.broadcast_to(seg, (LANES, seg.shape[1])))
    return seg


def key_window(seg_ref, seg_smem, i, block, run):
    length = seg_ref.shape[1]
    first = seg_smem[i * block].astype(f32)
    last = seg_smem[i * block + block - 1].astype(f32)
    seg = seg_ref[...]
    begin = jnp.sum(jnp.where(seg < first, 1.0, 0.0)).astype(jnp.int32) // LANES
    end = (jnp.sum(jnp.where(seg <= last, 1.0, 0.0)).astype(jnp.int32) + LANES - 1) // LANES
    need = (end - begin) * LANES
    smaller = 0
    for size in (length // 2, 3 * length // 4, length):

        @pl.when((need > smaller) & (need <= size))
        def _(size=size):
            start = jnp.minimum(begin, (length - size) // LANES)
            run(pl.multiple_of(start * LANES, LANES), size)

        smaller = size


def attn_forward_kernel(
    n_head, block, h_ref, segs_ref, x_ref, wq_ref, wk_ref, wv_ref, bq_ref, bv_ref, seg_ref, q_ref, k_ref, v_ref, m_ref,
    lt_ref, *refs
):
    pieces, (col_ref, row_ref) = refs[:n_head], refs[n_head:]
    length, width = q_ref.shape
    share = length // n_head
    x = x_ref[...]
    q_ref[...] = ((nn(x, wq_ref[...]) + bq_ref[...]) * 0.125).astype(bf16)
    k_ref[...] = nn(x, wk_ref[...]).astype(bf16)
    v_ref[...] = (nn(x, wv_ref[...]) + bv_ref[...]).astype(bf16)
    first = lax.broadcasted_iota(jnp.int32, (1, LANES), 1) < HEAD_DIM
    row_ref[...] = seg_columns(seg_ref, col_ref)

    def step(i, _):
        rows = rows_at(i, block)

        def run(start, size):
            keys = pl.ds(start, size)
            same = col_ref[rows, 0:1] == row_ref[:, keys]
            for pair in range(width // LANES):
                cols = slice(pair * LANES, (pair + 1) * LANES)
                q, k, v = q_ref[rows, cols], k_ref[keys, cols], v_ref[keys, cols]
                outs, tops = [], []
                for odd in range(2):
                    mine = jnp.logical_not(first) if odd else first
                    scores = jnp.where(same, nt(jnp.where(mine, q, jnp.zeros_like(q)), k), MASKED)
                    top = jnp.max(scores, -1, keepdims=True)
                    probs = jnp.exp(scores - top).astype(bf16)
                    outs.append(nn(probs, jnp.where(mine, v, jnp.ones_like(v))))
                    tops.append(top)
                total = jnp.where(first, outs[1], outs[0])
                mix = jnp.where(first, outs[0], outs[1]) / pltpu.roll(total, HEAD_DIM, 1)
                m_ref[rows, cols] = mix.astype(bf16)
                lt_ref[rows, cols] = jnp.where(first, tops[1], tops[0]) + jnp.log(total)

        key_window(row_ref, segs_ref, i, block, run)
        return 0

    lax.fori_loop(0, length // block, step, 0)
    h = h_ref[0]
    for k, piece in enumerate(pieces):
        piece[...] = m_ref[rows_at(h ^ k, share), :]


def attn_forward(h, segs, x, wq, wk, wv, bq, bv, seg_row, n_head, block=256):
    length, model = x.shape
    width = wq.shape[1]
    return call(
        functools.partial(attn_forward_kernel, n_head, block),
        "attention_forward",
        [shape((length, width), bf16)] * 4
        + [shape((length, width), f32)]
        + [shape((length // n_head, width), bf16)] * n_head,
        (h, segs, x, wq, wk, wv, bq, bv, seg_row),
        scalars=2,
        far=True,
        scratch=[pltpu.VMEM((length, LANES), f32), pltpu.VMEM((1, length), f32)],
        us=12,
    )


def attn_backward_kernel(n_head, block, h_ref, segs_ref, q_ref, k_ref, v_ref, m_ref, lt_ref, seg_ref, *refs):
    g_pieces, (out_ref, bias_ref) = refs[:n_head], refs[n_head : n_head + 2]
    g_ref, row_ref, col_ref, seg_row_ref, gk_ref, gv_ref = refs[n_head + 2 :]
    length, width = q_ref.shape
    share = length // n_head
    h = h_ref[0]
    for k, piece in enumerate(g_pieces):
        g_ref[rows_at(h ^ k, share), :] = piece[...]
    first = lax.broadcasted_iota(jnp.int32, (1, LANES), 1) < HEAD_DIM
    seg_row_ref[...] = seg_columns(seg_ref, col_ref)
    row_ref[0:width, :] = jnp.transpose(lt_ref[...])
    prod = g_ref[...].astype(f32) * m_ref[...].astype(f32)
    head = lax.broadcasted_iota(jnp.int32, (8, width), 0)
    col = lax.broadcasted_iota(jnp.int32, (8, width), 1)
    pick = jnp.where(col // HEAD_DIM == head, 1.0, 0.0).astype(bf16)
    high = prod.astype(bf16)
    low = (prod - high.astype(f32)).astype(bf16)
    row_ref[width : width + 8, :] = nt(pick, high) + nt(pick, low)
    gk_ref[...] = jnp.zeros_like(gk_ref)
    gv_ref[...] = jnp.zeros_like(gv_ref)

    def step(i, _):
        rows = rows_at(i, block)

        def run(start, size):
            keys = pl.ds(start, size)
            same = col_ref[keys, 0:1] == seg_row_ref[:, rows]
            for pair in range(width // LANES):
                cols = slice(pair * LANES, (pair + 1) * LANES)
                q, k, v, g = q_ref[rows, cols], k_ref[keys, cols], v_ref[keys, cols], g_ref[rows, cols]
                gq, gk, gv = jnp.zeros((block, LANES), f32), gk_ref[keys, cols], gv_ref[keys, cols]
                for odd in range(2):
                    mine = jnp.logical_not(first) if odd else first
                    place = pair * LANES + (0 if odd else HEAD_DIM)
                    log_total = row_ref[place : place + 1, rows]
                    inner = row_ref[width + 2 * pair + odd : width + 2 * pair + odd + 1, rows]
                    q_mine, g_mine = jnp.where(mine, q, jnp.zeros_like(q)), jnp.where(mine, g, jnp.zeros_like(g))
                    probs = jnp.exp(jnp.where(same, nt(k, q_mine), MASKED) - log_total)
                    gv = gv + nn(probs.astype(bf16), g_mine)
                    gs = (probs * (nt(v, g_mine) - inner)).astype(bf16)
                    gk = gk + nn(gs, q_mine)
                    gq = gq + tn(gs, jnp.where(mine, k, jnp.zeros_like(k)))
                gk_ref[keys, cols], gv_ref[keys, cols] = gk, gv
                out_ref[rows, cols] = gq.astype(bf16) * bf16(0.125)

        key_window(seg_row_ref, segs_ref, i, block, run)
        return 0

    lax.fori_loop(0, length // block, step, 0)
    out_ref[:, width : 2 * width] = gk_ref[...].astype(bf16)
    out_ref[:, 2 * width :] = gv_ref[...].astype(bf16)
    bias_ref[...] = jnp.zeros_like(bias_ref)
    bias_ref[0:1, 0:width] = column_sum(out_ref[:, :width].astype(f32))
    bias_ref[1:2, 0:width] = column_sum(out_ref[:, 2 * width :].astype(f32))


def attn_backward(h, segs, q, k, v, m, log_total, seg_row, grads, model, block=256):
    length, width = q.shape
    n_head = len(grads)
    return call(
        functools.partial(attn_backward_kernel, n_head, block),
        "attention_backward",
        [shape((length, 3 * width), bf16), shape((8, model), f32)],
        (h, segs, q, k, v, m, log_total, seg_row, *grads),
        scalars=2,
        far=True,
        scratch=[
            pltpu.VMEM((length, width), bf16),
            pltpu.VMEM((width + 8, length), f32),
            pltpu.VMEM((length, LANES), f32),
            pltpu.VMEM((1, length), f32),
            pltpu.VMEM((length, width), f32),
            pltpu.VMEM((length, width), f32),
        ],
        us=13,
        vmem=24,
    )


def mean(value):
    return jnp.mean(value, -1, keepdims=True)


def norm_back(grad, unit, inv, gain):
    gg = grad * gain
    return inv * (gg - mean(gg) - unit * mean(gg * unit))


def column_sum(value):
    return jnp.sum(value, 0, keepdims=True)


def slice_of(ref, k):
    if len(ref.shape) == 3:
        return ref[k]
    return jnp.concatenate([ref[i, k] for i in range(ref.shape[0])], 0)


def attn_out_kernel(n_head, x_ref, w_ref, bias_ref, gain_ref, shift_ref, *refs):
    pieces, (normed_ref, low_ref, unit_ref, inv_ref) = refs[:n_head], refs[n_head:]
    total = None
    for k, piece in enumerate(pieces):
        part = nn(piece[...], slice_of(w_ref, k)).astype(bf16).astype(f32)
        total = part if total is None else total + part
    pre = x_ref[...].astype(f32) + total + bias_ref[...]
    center = pre - mean(pre)
    inv = lax.rsqrt(mean(center * center) + NORM_EPS)
    unit = center * inv
    normed = unit * gain_ref[...] + shift_ref[...]
    normed_ref[...] = normed
    low_ref[...] = normed.astype(bf16)
    unit_ref[...] = unit
    inv_ref[...] = jnp.broadcast_to(inv, inv_ref.shape)


def attn_out(x_own, weight, vectors, pieces):
    share, model = x_own.shape
    return call(
        functools.partial(attn_out_kernel, len(pieces)),
        "attention_out_norm",
        [
            shape((share, model), f32),
            shape((share, model), bf16),
            shape((share, model), f32),
            shape((share, LANES), f32),
        ],
        (x_own, weight, *vectors, *pieces),
        us=1.5,
    )


def loss_kernel(h_ref, normed_ref, cot_ref, lexcot_ref, seg_ref, *refs):
    (down_b_ref, gain_ref, shift_ref, lexw_ref), refs = refs[:4], refs[4:]
    parts, (result_ref, lex_ref, grad_ref, low_ref, sums_ref, later_ref) = refs[:-6], refs[-6:]
    share, model = normed_ref.shape
    total = parts[0][...].astype(f32)
    for part in parts[1:]:
        total = total + part[...].astype(f32)
    pre = normed_ref[...] + total + down_b_ref[...]
    gain, lex_w = gain_ref[...], lexw_ref[...]
    center = pre - mean(pre)
    inv = lax.rsqrt(mean(center * center) + NORM_EPS)
    unit = center * inv
    final = unit * gain + shift_ref[...]
    result_ref[...] = final.astype(bf16)
    lex_cot = jnp.transpose(jnp.broadcast_to(lexcot_ref[...], (LANES, share)))[:, 0:1]
    lex_in = jnp.sum(final * lex_w, -1, keepdims=True)
    away = jnp.exp(-jnp.abs(lex_in))
    scale = lex_cot * (jnp.where(lex_in >= 0, 1.0, away) / (1.0 + away))
    lexical = jnp.maximum(lex_in, 0.0) + jnp.log1p(away)
    lex_row = jnp.transpose(jnp.broadcast_to(lexical, (share, LANES)))[0:8, :]
    lex_ref[...] = lex_row
    grad_final = cot_ref[...].astype(f32) + scale * lex_w
    grad = norm_back(grad_final, unit, inv, gain)
    grad_ref[...] = grad
    low_ref[...] = grad.astype(bf16)
    seg = jnp.broadcast_to(seg_ref[...].astype(f32), later_ref.shape)
    place = lax.broadcasted_iota(jnp.int32, later_ref.shape, 1)
    later_ref[...] = jnp.where((seg == pltpu.roll(seg, 1, 1)) & (place > 0), 1.0, 0.0)
    later = later_ref[0:1, rows_at(h_ref[0], share)]
    lane = lax.broadcasted_iota(jnp.int32, (1, model), 1)
    lex_sum = jnp.sum(lex_row[0:1, :] * later, -1, keepdims=True)
    count = jnp.sum(later, -1, keepdims=True)
    sums_ref[...] = jnp.zeros_like(sums_ref)
    sums_ref[0:1, :] = column_sum(grad)
    sums_ref[1:2, :] = column_sum(grad_final * unit)
    sums_ref[2:3, :] = column_sum(grad_final)
    sums_ref[3:4, :] = column_sum(scale * final)
    sums_ref[4:5, :] = jnp.where(lane == 0, lex_sum, 0.0) + jnp.where(lane == 1, count, 0.0)


def loss(h, normed, cotangent, lex_cot, seg_row, vectors, parts):
    share, model = normed.shape
    return call(
        loss_kernel,
        "loss_norm_back",
        [
            shape((share, model), bf16),
            shape((8, share), f32),
            shape((share, model), f32),
            shape((share, model), bf16),
            shape((8, model), f32),
        ],
        (h, normed, cotangent, lex_cot, seg_row, *vectors, *parts),
        scalars=1,
        scratch=[pltpu.VMEM((8, seg_row.shape[1]), f32)],
        us=2.5,
    )


def norm_one_back_kernel(n_head, grad_ref, unit_ref, inv_ref, gain_ref, w_ref, sums_two_ref, up_ref, *refs):
    n_out = 3 + n_head
    parts, outs = refs[: -n_out - 1], refs[-n_out - 1 : -1]
    pre_ref, low_ref, parts_ref = outs[:3]
    small_ref = refs[-1]
    grad = grad_ref[...]
    for part in parts:
        grad = grad + part[...].astype(f32)
    unit = unit_ref[...]
    pre = norm_back(grad, unit, inv_ref[:, 0:1], gain_ref[0:1, :])
    pre_ref[...] = pre
    low = pre.astype(bf16)
    low_ref[...] = low
    for k in range(n_head):
        outs[3 + k][...] = nt(low, slice_of(w_ref, k)).astype(bf16)
    small_ref[...] = jnp.zeros_like(small_ref)
    small_ref[0:5, :] = sums_two_ref[0:5, :]
    small_ref[5:6, :] = column_sum(pre)
    small_ref[6:7, :] = column_sum(grad * unit)
    small_ref[7:8, :] = column_sum(grad)
    small_ref[8:9, 0 : up_ref.shape[1]] = up_ref[...]
    small = small_ref[...]
    high = small.astype(bf16)
    parts_ref[0:SMALL, :] = high
    parts_ref[SMALL:, :] = (small - high.astype(f32)).astype(bf16)


def norm_one_back(grad, unit, inv, gain, weight, sums_two, up_sums, parts, n_head, width):
    share, model = grad.shape
    return call(
        functools.partial(norm_one_back_kernel, n_head),
        "norm_one_back",
        [shape((share, model), f32), shape((share, model), bf16), shape((2 * SMALL, model), bf16)]
        + [shape((share, width), bf16)] * n_head,
        (grad, unit, inv, gain, weight, sums_two, up_sums, *parts),
        scratch=[pltpu.VMEM((SMALL, model), f32)],
        us=1.5,
    )


def halves_order(count):
    if count == 1:
        return [0]
    evens = [2 * i for i in halves_order(count // 2)]
    return evens + [i + 1 for i in evens]


def input_grad_kernel(n_head, h_ref, grad_ref, *refs):
    weights, outs = refs[:3], refs[3:]
    share = 2 * outs[0].shape[0] // n_head
    width = weights[0].shape[1]
    for place, k in enumerate(halves_order(n_head)):
        rows = rows_at(h_ref[0] ^ k, share)
        total = None
        for i, weight in enumerate(weights):
            part = nt(grad_ref[rows, i * width : (i + 1) * width], weight[...])
            total = part if total is None else total + part
        side, at = divmod(place, n_head // 2)
        outs[side][at * share : (at + 1) * share, :] = total.astype(bf16)


def input_grad(h, grad, weights, n_head):
    length, model = grad.shape[0], weights[0].shape[0]
    return call(
        functools.partial(input_grad_kernel, n_head),
        "input_grad",
        [shape((length // 2, model), bf16)] * 2,
        (h, grad, *weights),
        scalars=1,
        us=2.5,
    )


def assemble_kernel(n_out, flag_ref, *refs):
    natives, pieces, outs = refs[:n_out], refs[n_out:-n_out], refs[-n_out:]

    @pl.when(flag_ref[0] == 1)
    def _():
        for native_ref, out_ref in zip(natives, outs):
            out_ref[...] = native_ref[...]

    @pl.when(flag_ref[0] == 0)
    def _():
        offset = 0
        for out_ref in outs:
            rows = out_ref.shape[0] // len(pieces)
            for k, piece in enumerate(pieces):
                out_ref[rows_at(flag_ref[1] ^ k, rows), :] = piece[offset : offset + rows, :]
            offset += rows


def assemble(flags, natives, pieces, name):
    return call(
        functools.partial(assemble_kernel, len(natives)),
        name,
        [shape(native.shape, bf16) for native in natives],
        (flags, *natives, *pieces),
        scalars=1,
    )


def ffn_forward_kernel(xa_ref, xb_ref, up_ref, bias_ref, down_ref, act_ref, slope_ref, pa_ref, pb_ref, acc_ref):
    share, units = xa_ref.shape[0], up_ref.shape[1]
    tile = min(TILE, units)
    x = jnp.concatenate([xa_ref[...], xb_ref[...]], 0)
    for j in range(units // tile):
        cols = slice(j * tile, (j + 1) * tile)
        hidden = nn(x, up_ref[:, cols]) + bias_ref[:, cols]
        below = 0.5 * (1.0 + lax.erf(hidden * math.sqrt(0.5)))
        active = (hidden * below).astype(bf16)
        act_ref[:, cols] = active
        slope_ref[:, cols] = (
            below + hidden * (jnp.exp(-0.5 * hidden * hidden) * (1.0 / math.sqrt(2 * math.pi)))
        ).astype(bf16)
        part = nn(active, down_ref[cols, :])
        if j == 0:
            acc_ref[...] = part
        else:
            acc_ref[...] += part
    pa_ref[...] = acc_ref[:share, :].astype(bf16)
    pb_ref[...] = acc_ref[share:, :].astype(bf16)


def ffn_forward(xa, xb, up, bias, down):
    share, model = xa.shape
    units = up.shape[1]
    return call(
        ffn_forward_kernel,
        "ffn_forward",
        [shape((2 * share, units), bf16)] * 2 + [shape((share, model), bf16)] * 2,
        (xa, xb, up, bias, down),
        scratch=[pltpu.VMEM((2 * share, model), f32)],
        us=4,
    )


def ffn_backward_kernel(ga_ref, gb_ref, up_ref, down_ref, slope_ref, gh_ref, pa_ref, pb_ref, sum_ref, acc_ref):
    share, units = ga_ref.shape[0], up_ref.shape[1]
    tile = min(TILE, units)
    grads = jnp.concatenate([ga_ref[...], gb_ref[...]], 0)
    sum_ref[...] = jnp.zeros_like(sum_ref)
    for j in range(units // tile):
        cols = slice(j * tile, (j + 1) * tile)
        gh = (nt(grads, down_ref[cols, :]) * slope_ref[:, cols].astype(f32)).astype(bf16)
        gh_ref[:, cols] = gh
        sum_ref[0:1, cols] = column_sum(gh.astype(f32))
        part = nt(gh, up_ref[:, cols])
        if j == 0:
            acc_ref[...] = part
        else:
            acc_ref[...] += part
    pa_ref[...] = acc_ref[:share, :].astype(bf16)
    pb_ref[...] = acc_ref[share:, :].astype(bf16)


def ffn_backward(ga, gb, up, down, slope):
    share, model = ga.shape
    units = up.shape[1]
    return call(
        ffn_backward_kernel,
        "ffn_backward",
        [shape((2 * share, units), bf16)] + [shape((share, model), bf16)] * 2 + [shape((8, units), f32)],
        (ga, gb, up, down, slope),
        scratch=[pltpu.VMEM((2 * share, model), f32)],
        us=3.3,
    )


def row_blocks(refs, count):
    each = count // len(refs)
    size = refs[0].shape[0] // each
    return [ref.at[s * size : (s + 1) * size, :] for ref in refs for s in range(each)]


def weight_grad_kernel(n_left, n_right, place, *refs):
    lefts, rights, rest = refs[:n_left], refs[n_left : n_left + n_right], refs[n_left + n_right :]
    count = max(n_left, n_right)
    lefts, rights = row_blocks(lefts, count), row_blocks(rights, count)
    rows = lefts[0].shape[1]
    tile = min(TILE, rows)
    for j in range(rows // tile):
        total = None
        for left, right in zip(lefts, rights):
            part = tn(left[:, j * tile : (j + 1) * tile], right[...])
            total = part if total is None else total + part
        place(j, total.astype(bf16), *rest)


def weight_grad(lefts, rights, name):
    rows, cols = lefts[0].shape[1], rights[0].shape[1]

    def place(j, value, out_ref):
        out_ref[j * value.shape[0] : (j + 1) * value.shape[0], :] = value

    return call(
        functools.partial(weight_grad_kernel, len(lefts), len(rights), place),
        name,
        shape((rows, cols), bf16),
        (*lefts, *rights),
        us=3,
    )


def widen(gathered):
    pieces, rows, cols = gathered.shape

    def kernel(in_ref, out_ref):
        out_ref[...] = in_ref[0].astype(f32)

    return pl.pallas_call(
        kernel,
        grid=(pieces,),
        in_specs=[pl.BlockSpec((1, rows, cols), lambda i: (i, 0, 0))],
        out_specs=pl.BlockSpec((rows, cols), lambda i: (i, 0)),
        out_shape=shape((pieces * rows, cols), f32),
        compiler_params=pltpu.CompilerParams(vmem_limit_bytes=58 * MIB),
        cost_estimate=pl.CostEstimate(flops=1000, bytes_accessed=100000, transcendentals=0),
        name="widen",
    )(gathered)


def grads_final(g, gathered, ffn_rows, out_rows, qkv_rows, tokens):
    n_batch, rows, model = gathered.shape
    chips = n_batch // 2
    width = n_batch * qkv_rows // 3

    def kernel(g_ref, in_ref, up_ref, out_ref, q_ref, k_ref, v_ref, *refs):
        row_refs, (query_b_ref, value_b_ref, mean_ref, share_ref, all_ref) = refs[:8], refs[8:]
        small = None
        shared = lax.broadcasted_iota(jnp.int32, (SMALL, 1), 0) != 8
        for b in range(n_batch):
            p, core = divmod(b, 2)
            up_ref[b * ffn_rows : (b + 1) * ffn_rows, :] = in_ref[b, :ffn_rows].astype(f32)
            at = ffn_rows
            start = (core * chips + p) * qkv_rows
            all_ref[start : start + qkv_rows, :] = in_ref[b, at : at + qkv_rows]
            at += qkv_rows
            out_ref[b * out_rows : (b + 1) * out_rows, :] = in_ref[b, at : at + out_rows].astype(f32)
            at += out_rows
            value = in_ref[b, at : at + SMALL].astype(f32) + in_ref[b, at + SMALL : at + 2 * SMALL].astype(f32)
            value = jnp.where(shared | (g_ref[0] == core), value, 0.0)
            small = value if small is None else small + value
        for i, ref in enumerate((q_ref, k_ref, v_ref)):
            ref[...] = jnp.transpose(all_ref[i * width : (i + 1) * width, :].astype(f32))
        for ref, at in zip(row_refs, (0, 1, 2, 3, 5, 6, 7, 8)):
            ref[...] = small[at : at + 1, :]
        query_b_ref[...] = small[9:10, :width]
        value_b_ref[...] = small[10:11, :width]
        count = small[4:5, 1:2]
        mean_ref[...] = small[4:5, 0:1] / count
        share_ref[...] = count / tokens

    flat = [(1, model)] * 8 + [(1, width)] * 2 + [(1, 1)] * 2
    return call(
        kernel,
        "grads_final",
        [shape((n_batch * ffn_rows, model), f32), shape((n_batch * out_rows, model), f32)]
        + [shape((model, width), f32)] * 3
        + [shape(dims, f32) for dims in flat],
        (g, gathered),
        scalars=1,
        far=True,
        scratch=[pltpu.VMEM((3 * width, model), bf16)],
    )


def out_grad(c, low, pieces, chips):
    model = low.shape[1]
    width, n_head = pieces[0].shape[1], len(pieces)
    rows = width // (2 * chips)

    def kernel(c_ref, low_ref, *refs):
        ins, (keep_ref, send_ref, all_ref) = refs[:n_head], refs[n_head:]
        c_now = c_ref[0]
        for k, piece in enumerate(ins):
            all_ref[...] = tn(piece[...], low_ref[...]).astype(bf16)
            for j in range(chips):
                to = slice((k * chips + j) * rows, (k * chips + j + 1) * rows)
                for ref, core in ((keep_ref, c_now), (send_ref, 1 - c_now)):
                    ref[to, :] = all_ref[pl.ds(pl.multiple_of((2 * j + core) * rows, rows), rows), :]

    return call(
        kernel,
        "out_weight_grad",
        [shape((n_head * chips * rows, model), bf16)] * 2,
        (c, low, *pieces),
        scalars=1,
        scratch=[pltpu.VMEM((width, model), bf16)],
        us=1,
    )


def qkv_grad(c, x, grad):
    rows, cols = grad.shape[1], x.shape[1]
    mid = rows // 2

    def kernel(c_ref, x_ref, grad_ref, keep_ref, send_ref, all_ref):
        tile = min(TILE, rows)
        for j in range(rows // tile):
            at = slice(j * tile, (j + 1) * tile)
            all_ref[at, :] = tn(grad_ref[:, at], x_ref[...]).astype(bf16)
        core = c_ref[0]
        keep_ref[...] = all_ref[rows_at(core, mid), :]
        send_ref[...] = all_ref[rows_at(1 - core, mid), :]

    return call(
        kernel,
        "qkv_weight_grad",
        [shape((mid, cols), bf16)] * 2,
        (c, x, grad),
        scalars=1,
        scratch=[pltpu.VMEM((rows, cols), bf16)],
        us=2,
    )


def fold(p, keep, got, blocks, order):
    chips = len(order)
    rows, cols = keep.shape
    size = rows // (blocks * chips)

    def kernel(p_ref, keep_ref, got_ref, first_ref, second_ref):
        for i, k in enumerate(order):
            out, place = (first_ref, i) if i < chips // 2 else (second_ref, i - chips // 2)
            for j in range(blocks):
                at = rows_at(j * chips + (p_ref[0] ^ k), size)
                total = keep_ref[at, :].astype(f32) + got_ref[at, :].astype(f32)
                to = (place * blocks + j) * size
                out[to : to + size, :] = total.astype(bf16)

    return call(
        kernel,
        "fold_cores",
        [shape((rows // 2, cols), bf16)] * 2,
        (p, keep, got),
        scalars=1,
        us=0.7,
    )


def build(n_batch, n_head):
    half = n_head // 2
    chips = n_batch // 2
    n_all = n_batch * n_head
    CORE = n_head
    CHIP = 2 * n_head

    def permute(value, mask, among=lambda i: True):
        return lax.ppermute(value, ALL, [(i, i ^ mask) for i in range(n_all) if among(i)])

    def after(value, *earlier):
        return lax.optimization_barrier((value, *earlier))[0]

    def is_native(i):
        return ((i // half) % 2) == ((i // n_head) % 2)

    def is_foreign(i):
        return not is_native(i)

    def rows_of(value, start, count):
        return lax.dynamic_slice_in_dim(value, start, count, 0)

    def exchange_slices(piece):
        return jnp.stack([piece] + [permute(piece, k) for k in range(1, n_head)])

    def bits(count):
        return [1 << i for i in reversed(range(count.bit_length() - 1))]

    def halve(value, masks):
        for mask in masks:
            mid = value.shape[0] // 2
            value = sum_of([value[:mid], permute(value[mid:], mask)])
        return value

    def sum_of(values):
        return sum(v.astype(f32) for v in values).astype(bf16)

    def group_stage(own, work, filler=None):
        fars = [permute(own, dl) for dl in range(1, half)]
        pairs = [(own, permute(own, CORE))]
        extra, near, other = work(0, *pairs[0])
        extras, fars_out, last, filled = [extra], [], near, None
        crossed = permute(other, CORE)
        for dl in range(1, half):
            far = after(fars[dl - 1], last)
            pairs.append((far, permute(far, CORE)))
            extra, mine, other = work(dl, *pairs[dl])
            extras.append(extra)
            other = permute(other, CORE)
            if filler and dl == half - 1:
                filled = filler(pairs, extras)
                other = after(other, filled)
            last = sum_of([mine, other])
            fars_out.append(permute(last, dl))
        return extras, pairs, [near, crossed] + fars_out, last, filled

    def on_device(
        inputs, segment_ids, query_weight, query_bias, key_weight, value_weight, value_bias, output_weight,
        output_bias, attn_gain, attn_shift, up_weight, up_bias, down_weight, down_bias, ffn_gain, ffn_shift,
        lexical_weight, out_cotangent, lexical_cotangent,
    ):
        length, model = inputs.shape
        share = out_cotangent.shape[0]
        width = query_weight.shape[1]
        units = up_weight.shape[1]
        pairs = width // LANES
        p, c, g, l = (lax.axis_index(a) for a in ALL)
        h = g * half + l
        b = p * 2 + c
        native = c == g
        scalar = lambda *values: jnp.stack([jnp.asarray(v, jnp.int32) for v in values])
        h_arr, c_arr, p_arr, where_arr = scalar(h), scalar(c), scalar(p), scalar(p, c)
        flags = scalar(native, p)
        row = lambda v: v.reshape(1, -1)
        seg_row = row(segment_ids)

        with jax.named_scope("fetch_weights"):
            up_size, down_size = model // chips, units // chips
            out_piece = width // n_batch
            joint = units == model and out_piece % 16 == 0 and chips == 4 and half == 2
            firsts = [rows_of(up_weight, p * up_size, up_size), rows_of(down_weight, p * down_size, down_size)]
            if joint:
                firsts = [jnp.concatenate(firsts, 0)]
            out_sent = after(rows_of(output_weight, b * out_piece, out_piece), *firsts)
            firsts = [permute(x, half, is_native) for x in firsts]
            out_parts = exchange_slices(out_sent)
            out_all = lax.all_gather(out_parts, PLANE, axis=0)
            if not joint:
                out_all = jnp.swapaxes(out_all, 0, 1).reshape(n_head, width, model)

        with jax.named_scope("attention"):
            *heads, mixed_own = (
                lambda q, k, v, m, lt, *pieces: (q, k, v, m, lt, list(pieces))
            )(
                *attn_forward(
                    h_arr, segment_ids, inputs, query_weight, key_weight, value_weight, row(query_bias),
                    row(value_bias), seg_row, n_head,
                )
            )
            mixed_first = mixed_own[0]
            mixed_own = [mixed_own[0]] + [permute(mixed_own[m], m) for m in range(1, n_head)]

        with jax.named_scope("fetch_weights"):
            fetched = []
            for x in firsts:
                x = after(x, mixed_first)
                got = [x] + [permute(x, CHIP * k, is_foreign) for k in range(1, min(chips, 3))]
                x = after(x, *mixed_own)
                fetched.append(got + [permute(x, CHIP * k, is_foreign) for k in range(3, chips)])
            bias_far = permute(after(up_bias, *mixed_own), half)

        with jax.named_scope("attention_out"):
            normed, normed_low, unit_one, inv_one = attn_out(
                rows_of(inputs, h * share, share),
                out_all,
                [row(output_bias), row(attn_gain), row(attn_shift)],
                mixed_own,
            )

        with jax.named_scope("ffn"):
            if joint:
                up_use, down_use = assemble(flags, [up_weight, down_weight], fetched[0], "assemble")
            else:
                up_use, down_use = (
                    assemble(flags, [w], got, "assemble")[0] for w, got in zip((up_weight, down_weight), fetched)
                )
            bias_use = row(jnp.where(native, up_bias, bias_far))

            def forward_work(dl, xa, xb):
                active, slope, pa, pb = ffn_forward(xa, xb, up_use, bias_use, down_use)
                return (active, slope), pa, pb

            extras, normed_all, ffn_parts, _, _ = group_stage(normed_low, forward_work)
            actives, slopes = [e[0] for e in extras], [e[1] for e in extras]

        with jax.named_scope("loss"):
            result, lexical, grad_pre_two, grad_two_low, sums_two = loss(
                h_arr,
                normed,
                out_cotangent,
                row(lexical_cotangent.astype(f32)),
                seg_row,
                [row(down_bias), row(ffn_gain), row(ffn_shift), row(lexical_weight)],
                ffn_parts,
            )

        flat = lambda values: [x for pair in values for x in pair]
        with jax.named_scope("ffn_back"):

            def backward_work(dl, ga, gb):
                grad_hidden, pa, pb, sums = ffn_backward(ga, gb, up_use, down_use, slopes[dl])
                return (grad_hidden, sums), pa, pb

            def down_grad(pairs, extras):
                return weight_grad([after(x, extras[-1][0]) for x in actives], flat(pairs), "down_weight_grad")

            extras, grad_two_all, normed_parts, last, grad_down = group_stage(grad_two_low, backward_work, down_grad)
            grad_hiddens = [e[0] for e in extras]
            up_b = sum(e[1][:1] for e in extras)

        with jax.named_scope("ffn_weight_grads"):
            down_part = lax.psum_scatter(grad_down, "p", scatter_dimension=0, tiled=True)
            grad_hiddens[-1] = after(grad_hiddens[-1], last)
            grad_up = weight_grad(flat(normed_all), grad_hiddens, "up_weight_grad")
            grad_up, *normed_parts = lax.optimization_barrier((grad_up, *normed_parts))
            up_part = lax.psum_scatter(grad_up, "p", scatter_dimension=0, tiled=True)

        with jax.named_scope("attention_out_back"):
            grad_pre_one, grad_one_low, small, *grad_mixed = norm_one_back(
                grad_pre_two, unit_one, inv_one, row(attn_gain), out_all, sums_two, up_b, normed_parts, n_head, width
            )
            grad_mixed = [grad_mixed[0]] + [permute(grad_mixed[m], m) for m in range(1, n_head)]

        q, k, v, m, log_total = heads
        scores_grad = lambda grads: attn_backward(
            h_arr, segment_ids, q, k, v, m, log_total, seg_row, grads, model
        )

        def deliver(part):
            mid = part.shape[0] // 2
            this, that = rows_of(part, c * mid, mid), rows_of(part, (1 - c) * mid, mid)
            return this, permute(that, CORE, is_native), permute(this, half, is_foreign), permute(that, half | CORE, is_foreign)

        def delivered(this, beside, straight, crossed):
            return sum_of([jnp.where(native, this, beside), jnp.where(native, straight, crossed)])

        hold = lax.optimization_barrier
        if joint:
            with jax.named_scope("out_weight_grad"):
                out_keep, out_send = out_grad(c_arr, grad_one_low, mixed_own, chips)
                out_got, *grad_mixed = hold((permute(out_send, CORE), *grad_mixed))
                first, second = fold(p_arr, out_keep, out_got, n_head, range(chips))
                out_got = permute(second, CHIP * 2)
            with jax.named_scope("ffn_weight_grads"):
                down_sent = deliver(after(down_part, grad_mixed[-1]))
                grad_mixed[0], first, *down_sent = *hold((grad_mixed[0], first, down_sent[0])), *down_sent[1:]
            with jax.named_scope("attention_back"):
                grad_qkv, bias_sums = scores_grad(grad_mixed)
                out_got, grad_qkv, bias_sums, *down_sent = hold((out_got, grad_qkv, bias_sums, *down_sent))
            with jax.named_scope("ffn_weight_grads"):
                down_sum = delivered(*down_sent)
                down_all = lax.all_gather(down_sum, PLANE, axis=0)
            with jax.named_scope("out_weight_grad"):
                out_sum = sum_of([first, out_got])
                n = out_sum.shape[0] // 2
                out_got = permute(out_sum[n:], CHIP)
            with jax.named_scope("qkv_weight_grad"):
                keep, send = qkv_grad(c_arr, inputs, after(grad_qkv, out_sum, down_sum))
                got = permute(send, CORE)
            with jax.named_scope("input_grad"):
                in_keep, in_send = input_grad(
                    h_arr, after(grad_qkv, keep), (query_weight, key_weight, value_weight), n_head
                )
                in_got = permute(in_send, 1)
            with jax.named_scope("out_weight_grad"):
                out_sum = sum_of([out_sum[:n], after(out_got, in_keep)]).reshape(n_head, out_piece, model)
                line = [permute(jnp.concatenate([out_sum[i], small], 0), i) for i in range(1, n_head)]
            with jax.named_scope("qkv_weight_grad"):
                first, second = fold(p_arr, keep, after(got, out_sum), 1, halves_order(chips))
                got = permute(second, CHIP)
            with jax.named_scope("ffn_weight_grads"):
                up_part, got, in_got, *line = hold((up_part, got, in_got, *line))
                up_sent = deliver(up_part)
            with jax.named_scope("qkv_weight_grad"):
                piece = halve(sum_of([first, got]), [CHIP * 2])
            with jax.named_scope("ffn_weight_grads"):
                up_sum = delivered(*up_sent)
            with jax.named_scope("small_grads"):
                out_sum = sum_of([out_sum[0]] + [x[:out_piece] for x in line])
                own, one, two, three = (
                    x[:SMALL].astype(f32) + x[SMALL:].astype(f32) for x in [small] + [x[out_piece:] for x in line]
                )
                pack = jnp.concatenate(
                    [((own + two) + (one + three))[:8], (own + two)[8:9], bias_sums[: SMALL - 9]], 0
                )
            with jax.named_scope("gather_grads"):
                high = lax.reduce_precision(pack, 8, 7)
                sent = [up_sum, piece, out_sum, high.astype(bf16), (pack - high).astype(bf16)]
                *sent, in_got = hold((*sent, in_got))
                gathered = lax.all_gather(jnp.concatenate(sent, 0), PLANE, axis=0)
                grad_down_w = widen(after(down_all, sent[0]))
                grad_up_w, grad_out_w, grad_query_w, grad_key_w, grad_value_w, *rest = grads_final(
                    scalar(g), gathered, model // n_batch, out_piece, piece.shape[0], length * n_batch
                )
                down_b, ffn_g, ffn_s, lex_w, out_b, attn_g, attn_s, up_b = (x.reshape(-1) for x in rest[:8])
                query_b, value_b, mean_lexical, active_share = (x.reshape(-1) for x in rest[8:])
                mean_lexical, active_share = mean_lexical.reshape(()), active_share.reshape(())
        else:
            with jax.named_scope("attention_back"):
                grad_qkv, bias_sums = scores_grad(grad_mixed)
                in_keep, in_send = input_grad(h_arr, grad_qkv, (query_weight, key_weight, value_weight), n_head)
                in_got = permute(in_send, 1)
            with jax.named_scope("weight_grads"):
                grad_down_w, grad_up_w = (
                    lax.all_gather(delivered(*deliver(x)), PLANE, axis=0, tiled=True).astype(f32)
                    for x in (down_part, up_part)
                )
                parts = [tn(x, grad_one_low).astype(bf16) for x in mixed_own]
                out_sum = sum_of([parts[0]] + [permute(parts[m], m) for m in range(1, n_head)])
                grad_out_w = lax.psum(out_sum, PLANE).astype(f32)
                grad_qkv_w = lax.psum(tn(inputs, grad_qkv).astype(bf16), PLANE).astype(f32)
                grad_query_w, grad_key_w, grad_value_w = jnp.split(grad_qkv_w, 3, 1)
            with jax.named_scope("small_grads"):
                pack = small[:SMALL].astype(f32) + small[SMALL:].astype(f32)
                up_b = lax.psum(pack[8], ("p", "g"))
                up_b = jnp.where(native, up_b, permute(up_b, CORE))[:units]
                pack, biases = lax.psum(pack[:8], ALL), lax.psum(bias_sums, PLANE)
                down_b, ffn_g, ffn_s, lex_w, scalars, out_b, attn_g, attn_s = pack
                query_b, value_b = biases[0, :width], biases[1, :width]
                mean_lexical, active_share = scalars[0] / scalars[1], scalars[1] / (length * n_batch)

        with jax.named_scope("input_grad"):
            parts = sum_of([in_keep, in_got])
            bit = 2
            while bit < half:
                parts = halve(parts, [bit])
                bit *= 2
            mid = parts.shape[0] // 2
            far = permute(parts[mid:], half)
            far, grad_down_w = hold((far, grad_down_w))
            grad_inputs = (grad_pre_one + parts[:mid].astype(f32) + far.astype(f32)).astype(bf16)

        return (
            result,
            lexical[0],
            grad_inputs,
            grad_query_w,
            query_b,
            grad_key_w,
            grad_value_w,
            value_b,
            grad_out_w,
            out_b,
            attn_g,
            attn_s,
            grad_up_w,
            up_b,
            grad_down_w,
            down_b,
            ffn_g,
            ffn_s,
            lex_w,
            mean_lexical,
            active_share,
        )

    return on_device


def solution(mesh):
    n_batch, n_head = mesh.shape["batch"], mesh.shape["head"]
    fine = Mesh(mesh.devices.reshape(n_batch // 2, 2, 2, n_head // 2), ALL)
    line, tokens = P(LINE), P(ALL)
    rows, columns, whole = P(LINE, None), P(None, LINE), P()
    return jax.shard_map(
        build(n_batch, n_head),
        mesh=fine,
        in_specs=(
            P(PLANE, None), P(PLANE), columns, line, columns, columns, line, rows, whole, whole, whole, columns, line,
            rows, whole, whole, whole, whole, P(ALL, None), tokens,
        ),
        out_specs=(
            P(ALL, None), tokens, P(ALL, None), columns, line, columns, columns, line, rows, whole, whole, whole,
            columns, line, rows, whole, whole, whole, whole, whole, whole,
        ),
        check_vma=False,
    )
```

```python
import functools
import math

import jax
import jax.numpy as jnp
from jax import lax
from jax.experimental import pallas as pl
from jax.experimental.pallas import tpu as pltpu
from jax.sharding import Mesh, PartitionSpec as P

HEAD_DIM = 64
LANES = 128
TILE = 256
SMALL = 16
NORM_EPS = 1e-05
MASKED = -1000000000.0
ALL = ("p", "c", "g", "l")
PLANE = ("p", "c")
LINE = ("g", "l")
f32 = jnp.float32
bf16 = jnp.bfloat16
MIB = 2**20
VMEM = pl.BlockSpec(memory_space=pltpu.VMEM)
SMEM = pl.BlockSpec(memory_space=pltpu.SMEM)
HBM = pl.BlockSpec(memory_space=pltpu.HBM)


def shape(dims, dtype):
    return jax.ShapeDtypeStruct(dims, dtype)


def nn(left, right):
    return jnp.dot(left, right, preferred_element_type=f32)


def nt(left, right):
    return lax.dot_general(left, right, (((1,), (1,)), ((), ())), preferred_element_type=f32)


def tn(left, right):
    return lax.dot_general(left, right, (((0,), (0,)), ((), ())), preferred_element_type=f32)


def call(kernel, name, out_shape, args, scalars=0, scratch=(), us=1.0, vmem=12, far=False, cols=None):
    many = isinstance(out_shape, (list, tuple))
    outs = list(out_shape) if many else [out_shape]
    n_in, n_out = len(args), len(outs)
    far_in = range(scalars, n_in) if far else ()
    far_out = range(n_out) if far else ()
    cols = cols or {}
    held = [pltpu.VMEM(args[i].shape[:-1] + ((LANES,) if i in cols else args[i].shape[-1:]), args[i].dtype) for i in far_in]
    held += [pltpu.VMEM(outs[i].shape, outs[i].dtype) for i in far_out]
    n_held = len(held)

    def whole(*refs):
        given, extra = refs[: n_in + n_out], refs[n_in + n_out :]
        use = list(given)
        own, rest = extra[:n_held], extra[n_held:]
        if n_held:
            rest, sems = rest[:-1], rest[-1]
        copies = []
        for slot, i in enumerate(far_in):
            source = given[i]
            if i in cols:
                source = source.at[:, cols[i]]
            copies.append(pltpu.make_async_copy(source, own[slot], sems.at[slot]))
            use[i] = own[slot]
        for copy in copies:
            copy.start()
        for copy in copies:
            copy.wait()
        for slot, i in enumerate(far_out, len(far_in)):
            use[n_in + i] = own[slot]
        kernel(*use, *rest)
        copies = [
            pltpu.make_async_copy(own[slot], given[n_in + i], sems.at[slot]) for slot, i in enumerate(far_out, len(far_in))
        ]
        for copy in copies:
            copy.start()
        for copy in copies:
            copy.wait()

    place = HBM if far else VMEM
    result = pl.pallas_call(
        whole if n_held else kernel,
        out_shape=outs,
        in_specs=[SMEM] * scalars + [place] * (n_in - scalars),
        out_specs=[place] * n_out,
        scratch_shapes=held + list(scratch) + ([pltpu.SemaphoreType.DMA((n_held,))] if n_held else []),
        compiler_params=pltpu.CompilerParams(vmem_limit_bytes=(58 if far else vmem) * MIB),
        cost_estimate=pl.CostEstimate(flops=int(us * 1.1e7), bytes_accessed=int(us * 3.6e4), transcendentals=0),
        name=name,
    )(*args)
    return list(result) if many else result[0]


def rows_at(index, count):
    return pl.ds(pl.multiple_of(index * count, count), count)


def seg_columns(seg_ref, col_ref):
    seg = seg_ref[...].astype(f32)
    col_ref[...] = jnp.transpose(jnp.broadcast_to(seg, (LANES, seg.shape[1])))
    return seg


def key_window(seg_ref, seg_smem, i, block, run):
    length = seg_ref.shape[1]
    first = seg_smem[i * block].astype(f32)
    last = seg_smem[i * block + block - 1].astype(f32)
    seg = seg_ref[...]
    begin = jnp.sum(jnp.where(seg < first, 1.0, 0.0)).astype(jnp.int32) // LANES
    end = (jnp.sum(jnp.where(seg <= last, 1.0, 0.0)).astype(jnp.int32) + LANES - 1) // LANES
    need = (end - begin) * LANES
    smaller = 0
    for size in (length // 2, 3 * length // 4, length):

        @pl.when((need > smaller) & (need <= size))
        def _(size=size):
            start = jnp.minimum(begin, (length - size) // LANES)
            run(pl.multiple_of(start * LANES, LANES), size)

        smaller = size


def attn_forward_kernel(
    n_head, block, h_ref, segs_ref, x_ref, wq_ref, wk_ref, wv_ref, bq_ref, bv_ref, seg_ref, q_ref, k_ref, v_ref, m_ref,
    lt_ref, *refs
):
    pieces, (col_ref, row_ref) = refs[:n_head], refs[n_head:]
    length, width = q_ref.shape
    share = length // n_head
    x = x_ref[...]
    q_ref[...] = ((nn(x, wq_ref[...]) + bq_ref[...]) * 0.125).astype(bf16)
    k_ref[...] = nn(x, wk_ref[...]).astype(bf16)
    v_ref[...] = (nn(x, wv_ref[...]) + bv_ref[...]).astype(bf16)
    first = lax.broadcasted_iota(jnp.int32, (1, LANES), 1) < HEAD_DIM
    row_ref[...] = seg_columns(seg_ref, col_ref)

    def step(i, _):
        rows = rows_at(i, block)

        def run(start, size):
            keys = pl.ds(start, size)
            same = col_ref[rows, 0:1] == row_ref[:, keys]
            for pair in range(width // LANES):
                cols = slice(pair * LANES, (pair + 1) * LANES)
                q, k, v = q_ref[rows, cols], k_ref[keys, cols], v_ref[keys, cols]
                outs, tops = [], []
                for odd in range(2):
                    mine = jnp.logical_not(first) if odd else first
                    scores = jnp.where(same, nt(jnp.where(mine, q, jnp.zeros_like(q)), k), MASKED)
                    top = jnp.max(scores, -1, keepdims=True)
                    probs = jnp.exp(scores - top).astype(bf16)
                    outs.append(nn(probs, jnp.where(mine, v, jnp.ones_like(v))))
                    tops.append(top)
                total = jnp.where(first, outs[1], outs[0])
                mix = jnp.where(first, outs[0], outs[1]) / pltpu.roll(total, HEAD_DIM, 1)
                m_ref[rows, cols] = mix.astype(bf16)
                lt_ref[rows, cols] = jnp.where(first, tops[1], tops[0]) + jnp.log(total)

        key_window(row_ref, segs_ref, i, block, run)
        return 0

    lax.fori_loop(0, length // block, step, 0)
    h = h_ref[0]
    for k, piece in enumerate(pieces):
        piece[...] = m_ref[rows_at(h ^ k, share), :]


def attn_forward(h, segs, x, wq, wk, wv, bq, bv, seg_row, n_head, block=256):
    length, model = x.shape
    width = wq.shape[1]
    return call(
        functools.partial(attn_forward_kernel, n_head, block),
        "attention_forward",
        [shape((length, width), bf16)] * 4
        + [shape((length, width), f32)]
        + [shape((length // n_head, width), bf16)] * n_head,
        (h, segs, x, wq, wk, wv, bq, bv, seg_row),
        scalars=2,
        far=True,
        scratch=[pltpu.VMEM((length, LANES), f32), pltpu.VMEM((1, length), f32)],
        us=12,
    )


def attn_backward_kernel(n_head, block, where_ref, segs_ref, q_ref, k_ref, v_ref, m_ref, lt_ref, seg_ref, *refs):
    g_pieces, refs = refs[:n_head], refs[n_head:]
    x_ref, weights, bias_ref, in_keep_ref, in_send_ref, keep_ref, send_ref = refs[0], refs[1:4], *refs[4:9]
    g_ref, row_ref, col_ref, seg_row_ref, gk_ref, gv_ref, out_ref, all_ref = refs[9:]
    h_ref = where_ref
    length, width = q_ref.shape
    share = length // n_head
    h = h_ref[0]
    for k, piece in enumerate(g_pieces):
        g_ref[rows_at(h ^ k, share), :] = piece[...]
    first = lax.broadcasted_iota(jnp.int32, (1, LANES), 1) < HEAD_DIM
    seg_row_ref[...] = seg_columns(seg_ref, col_ref)
    row_ref[0:width, :] = jnp.transpose(lt_ref[...])
    prod = g_ref[...].astype(f32) * m_ref[...].astype(f32)
    head = lax.broadcasted_iota(jnp.int32, (8, width), 0)
    col = lax.broadcasted_iota(jnp.int32, (8, width), 1)
    pick = jnp.where(col // HEAD_DIM == head, 1.0, 0.0).astype(bf16)
    high = prod.astype(bf16)
    low = (prod - high.astype(f32)).astype(bf16)
    row_ref[width : width + 8, :] = nt(pick, high) + nt(pick, low)
    gk_ref[...] = jnp.zeros_like(gk_ref)
    gv_ref[...] = jnp.zeros_like(gv_ref)

    def step(i, _):
        rows = rows_at(i, block)

        def run(start, size):
            keys = pl.ds(start, size)
            same = col_ref[keys, 0:1] == seg_row_ref[:, rows]
            for pair in range(width // LANES):
                cols = slice(pair * LANES, (pair + 1) * LANES)
                q, k, v, g = q_ref[rows, cols], k_ref[keys, cols], v_ref[keys, cols], g_ref[rows, cols]
                gq, gk, gv = jnp.zeros((block, LANES), f32), gk_ref[keys, cols], gv_ref[keys, cols]
                for odd in range(2):
                    mine = jnp.logical_not(first) if odd else first
                    place = pair * LANES + (0 if odd else HEAD_DIM)
                    log_total = row_ref[place : place + 1, rows]
                    inner = row_ref[width + 2 * pair + odd : width + 2 * pair + odd + 1, rows]
                    q_mine, g_mine = jnp.where(mine, q, jnp.zeros_like(q)), jnp.where(mine, g, jnp.zeros_like(g))
                    probs = jnp.exp(jnp.where(same, nt(k, q_mine), MASKED) - log_total)
                    gv = gv + nn(probs.astype(bf16), g_mine)
                    gs = (probs * (nt(v, g_mine) - inner)).astype(bf16)
                    gk = gk + nn(gs, q_mine)
                    gq = gq + tn(gs, jnp.where(mine, k, jnp.zeros_like(k)))
                gk_ref[keys, cols], gv_ref[keys, cols] = gk, gv
                out_ref[rows, cols] = gq.astype(bf16) * bf16(0.125)

        key_window(seg_row_ref, segs_ref, i, block, run)
        return 0

    lax.fori_loop(0, length // block, step, 0)
    out_ref[:, width : 2 * width] = gk_ref[...].astype(bf16)
    out_ref[:, 2 * width :] = gv_ref[...].astype(bf16)
    bias_ref[...] = jnp.zeros_like(bias_ref)
    bias_ref[0:1, 0:width] = column_sum(out_ref[:, :width].astype(f32))
    bias_ref[1:2, 0:width] = column_sum(out_ref[:, 2 * width :].astype(f32))
    for place, k in enumerate(halves_order(n_head)):
        rows = rows_at(h ^ k, share)
        total = None
        for i, weight in enumerate(weights):
            part = nt(out_ref[rows, i * width : (i + 1) * width], weight[...])
            total = part if total is None else total + part
        side, at = divmod(place, n_head // 2)
        (in_keep_ref, in_send_ref)[side][at * share : (at + 1) * share, :] = total.astype(bf16)
    tile = min(TILE, 3 * width)
    for j in range(3 * width // tile):
        at = slice(j * tile, (j + 1) * tile)
        all_ref[at, :] = tn(out_ref[:, at], x_ref[...]).astype(bf16)
    mid = 3 * width // 2
    keep_ref[...] = all_ref[rows_at(where_ref[1], mid), :]
    send_ref[...] = all_ref[rows_at(1 - where_ref[1], mid), :]


def halves_order(count):
    if count == 1:
        return [0]
    evens = [2 * i for i in halves_order(count // 2)]
    return evens + [i + 1 for i in evens]


def attn_backward(where, segs, q, k, v, m, log_total, seg_row, grads, x, weights, block=256):
    length, width = q.shape
    model = x.shape[1]
    n_head = len(grads)
    return call(
        functools.partial(attn_backward_kernel, n_head, block),
        "attention_backward",
        [shape((8, model), f32)]
        + [shape((length // 2, model), bf16)] * 2
        + [shape((3 * width // 2, model), bf16)] * 2,
        (where, segs, q, k, v, m, log_total, seg_row, *grads, x, *weights),
        scalars=2,
        far=True,
        scratch=[
            pltpu.VMEM((length, width), bf16),
            pltpu.VMEM((width + 8, length), f32),
            pltpu.VMEM((length, LANES), f32),
            pltpu.VMEM((1, length), f32),
            pltpu.VMEM((length, width), f32),
            pltpu.VMEM((length, width), f32),
            pltpu.VMEM((length, 3 * width), bf16),
            pltpu.VMEM((3 * width, model), bf16),
        ],
        us=18,
    )


def mean(value):
    return jnp.mean(value, -1, keepdims=True)


def norm_back(grad, unit, inv, gain):
    gg = grad * gain
    return inv * (gg - mean(gg) - unit * mean(gg * unit))


def column_sum(value):
    return jnp.sum(value, 0, keepdims=True)


def slice_of(ref, k):
    if len(ref.shape) == 3:
        return ref[k]
    return jnp.concatenate([ref[i, k] for i in range(ref.shape[0])], 0)


def attn_out_kernel(n_head, x_ref, w_ref, bias_ref, gain_ref, shift_ref, *refs):
    pieces, (normed_ref, low_ref, unit_ref, inv_ref) = refs[:n_head], refs[n_head:]
    total = None
    for k, piece in enumerate(pieces):
        part = nn(piece[...], slice_of(w_ref, k)).astype(bf16).astype(f32)
        total = part if total is None else total + part
    pre = x_ref[...].astype(f32) + total + bias_ref[...]
    center = pre - mean(pre)
    inv = lax.rsqrt(mean(center * center) + NORM_EPS)
    unit = center * inv
    normed = unit * gain_ref[...] + shift_ref[...]
    normed_ref[...] = normed
    low_ref[...] = normed.astype(bf16)
    unit_ref[...] = unit
    inv_ref[...] = jnp.broadcast_to(inv, inv_ref.shape)


def attn_out(x_own, weight, vectors, pieces):
    share, model = x_own.shape
    return call(
        functools.partial(attn_out_kernel, len(pieces)),
        "attention_out_norm",
        [
            shape((share, model), f32),
            shape((share, model), bf16),
            shape((share, model), f32),
            shape((share, LANES), f32),
        ],
        (x_own, weight, *vectors, *pieces),
        us=1.5,
    )


def loss_kernel(h_ref, normed_ref, cot_ref, lexcot_ref, seg_ref, *refs):
    (down_b_ref, gain_ref, shift_ref, lexw_ref), refs = refs[:4], refs[4:]
    parts, (result_ref, lex_ref, grad_ref, low_ref, sums_ref, later_ref) = refs[:-6], refs[-6:]
    share, model = normed_ref.shape
    total = parts[0][...].astype(f32)
    for part in parts[1:]:
        total = total + part[...].astype(f32)
    pre = normed_ref[...] + total + down_b_ref[...]
    gain, lex_w = gain_ref[...], lexw_ref[...]
    center = pre - mean(pre)
    inv = lax.rsqrt(mean(center * center) + NORM_EPS)
    unit = center * inv
    final = unit * gain + shift_ref[...]
    result_ref[...] = final.astype(bf16)
    lex_cot = jnp.transpose(jnp.broadcast_to(lexcot_ref[...], (LANES, share)))[:, 0:1]
    lex_in = jnp.sum(final * lex_w, -1, keepdims=True)
    away = jnp.exp(-jnp.abs(lex_in))
    scale = lex_cot * (jnp.where(lex_in >= 0, 1.0, away) / (1.0 + away))
    lexical = jnp.maximum(lex_in, 0.0) + jnp.log1p(away)
    lex_row = jnp.transpose(jnp.broadcast_to(lexical, (share, LANES)))[0:8, :]
    lex_ref[...] = lex_row
    grad_final = cot_ref[...].astype(f32) + scale * lex_w
    grad = norm_back(grad_final, unit, inv, gain)
    grad_ref[...] = grad
    low_ref[...] = grad.astype(bf16)
    seg = jnp.broadcast_to(seg_ref[...].astype(f32), later_ref.shape)
    place = lax.broadcasted_iota(jnp.int32, later_ref.shape, 1)
    later_ref[...] = jnp.where((seg == pltpu.roll(seg, 1, 1)) & (place > 0), 1.0, 0.0)
    later = later_ref[0:1, rows_at(h_ref[0], share)]
    lane = lax.broadcasted_iota(jnp.int32, (1, model), 1)
    lex_sum = jnp.sum(lex_row[0:1, :] * later, -1, keepdims=True)
    count = jnp.sum(later, -1, keepdims=True)
    sums_ref[...] = jnp.zeros_like(sums_ref)
    sums_ref[0:1, :] = column_sum(grad)
    sums_ref[1:2, :] = column_sum(grad_final * unit)
    sums_ref[2:3, :] = column_sum(grad_final)
    sums_ref[3:4, :] = column_sum(scale * final)
    sums_ref[4:5, :] = jnp.where(lane == 0, lex_sum, 0.0) + jnp.where(lane == 1, count, 0.0)


def loss(h, normed, cotangent, lex_cot, seg_row, vectors, parts):
    share, model = normed.shape
    return call(
        loss_kernel,
        "loss_norm_back",
        [
            shape((share, model), bf16),
            shape((8, share), f32),
            shape((share, model), f32),
            shape((share, model), bf16),
            shape((8, model), f32),
        ],
        (h, normed, cotangent, lex_cot, seg_row, *vectors, *parts),
        scalars=1,
        scratch=[pltpu.VMEM((8, seg_row.shape[1]), f32)],
        us=2.5,
    )


def norm_one_back_kernel(n_head, grad_ref, unit_ref, inv_ref, gain_ref, w_ref, sums_two_ref, up_ref, *refs):
    n_out = 3 + n_head
    parts, outs = refs[: -n_out - 1], refs[-n_out - 1 : -1]
    pre_ref, low_ref, parts_ref = outs[:3]
    small_ref = refs[-1]
    grad = grad_ref[...]
    for part in parts:
        grad = grad + part[...].astype(f32)
    unit = unit_ref[...]
    pre = norm_back(grad, unit, inv_ref[:, 0:1], gain_ref[0:1, :])
    pre_ref[...] = pre
    low = pre.astype(bf16)
    low_ref[...] = low
    for k in range(n_head):
        outs[3 + k][...] = nt(low, slice_of(w_ref, k)).astype(bf16)
    small_ref[...] = jnp.zeros_like(small_ref)
    small_ref[0:5, :] = sums_two_ref[0:5, :]
    small_ref[5:6, :] = column_sum(pre)
    small_ref[6:7, :] = column_sum(grad * unit)
    small_ref[7:8, :] = column_sum(grad)
    small_ref[8:9, 0 : up_ref.shape[1]] = up_ref[...]
    parts_ref[...] = small_ref[...].astype(bf16)


def norm_one_back(grad, unit, inv, gain, weight, sums_two, up_sums, parts, n_head, width):
    share, model = grad.shape
    return call(
        functools.partial(norm_one_back_kernel, n_head),
        "norm_one_back",
        [shape((share, model), f32), shape((share, model), bf16), shape((SMALL, model), bf16)]
        + [shape((share, width), bf16)] * n_head,
        (grad, unit, inv, gain, weight, sums_two, up_sums, *parts),
        far=True,
        scratch=[pltpu.VMEM((SMALL, model), f32)],
        us=1.5,
    )


def assemble(flags, natives, pieces, name, bias=None):
    n_in, n_pieces = len(natives), len(pieces)
    args = [*natives, *pieces] + ([bias.reshape(1, -1)] if bias is not None else [])

    def kernel(flag_ref, *refs):
        own, parts, outs = refs[:n_in], refs[n_in : n_in + n_pieces], refs[len(args) : -2]
        tail_ref, sems = refs[-2:]

        def run(copies):
            for copy in copies:
                copy.start()
            for copy in copies:
                copy.wait()

        @pl.when(flag_ref[0] == 1)
        def _():
            run([pltpu.make_async_copy(own[i], outs[i], sems.at[i]) for i in range(n_in)])
            if bias is not None:
                outs[n_in][...] = refs[len(args) - 1][...]

        @pl.when(flag_ref[0] == 0)
        def _():
            copies, offset = [], 0
            for out_ref in outs[:n_in]:
                rows = out_ref.shape[0] // n_pieces
                for k, piece in enumerate(parts):
                    source = piece.at[offset : offset + rows, :]
                    target = out_ref.at[rows_at(flag_ref[1] ^ k, rows), :]
                    copies.append(pltpu.make_async_copy(source, target, sems.at[len(copies)]))
                offset += rows
            if bias is not None:
                copies.append(pltpu.make_async_copy(parts[0].at[offset : offset + SMALL, :], tail_ref, sems.at[len(copies)]))
            run(copies)
            if bias is not None:
                rows = tail_ref[...].astype(f32)
                outs[n_in][...] = rows[0:1] + rows[1:2] + rows[2:3]

    out_shape = [shape(native.shape, bf16) for native in natives]
    out_shape += [shape((1, bias.shape[0]), f32)] if bias is not None else []
    return list(
        pl.pallas_call(
            kernel,
            out_shape=out_shape,
            in_specs=[SMEM] + [HBM] * (n_in + n_pieces) + ([VMEM] if bias is not None else []),
            out_specs=[VMEM] * len(out_shape),
            scratch_shapes=[
                pltpu.VMEM((SMALL, pieces[0].shape[1]), bf16),
                pltpu.SemaphoreType.DMA((n_in * n_pieces + 1,)),
            ],
            compiler_params=pltpu.CompilerParams(vmem_limit_bytes=12 * MIB),
            cost_estimate=pl.CostEstimate(flops=1000, bytes_accessed=100000, transcendentals=0),
            name=name,
        )(flags, *args)
    )


def ffn_forward_kernel(xa_ref, xb_ref, up_ref, bias_ref, down_ref, act_ref, slope_ref, pa_ref, pb_ref, acc_ref):
    share, units = xa_ref.shape[0], up_ref.shape[1]
    tile = min(TILE, units)
    x = jnp.concatenate([xa_ref[...], xb_ref[...]], 0)
    for j in range(units // tile):
        cols = slice(j * tile, (j + 1) * tile)
        hidden = nn(x, up_ref[:, cols]) + bias_ref[:, cols]
        below = 0.5 * (1.0 + lax.erf(hidden * math.sqrt(0.5)))
        active = (hidden * below).astype(bf16)
        act_ref[:, cols] = active
        slope_ref[:, cols] = (
            below + hidden * (jnp.exp(-0.5 * hidden * hidden) * (1.0 / math.sqrt(2 * math.pi)))
        ).astype(bf16)
        part = nn(active, down_ref[cols, :])
        if j == 0:
            acc_ref[...] = part
        else:
            acc_ref[...] += part
    pa_ref[...] = acc_ref[:share, :].astype(bf16)
    pb_ref[...] = acc_ref[share:, :].astype(bf16)


def ffn_forward(xa, xb, up, bias, down):
    share, model = xa.shape
    units = up.shape[1]
    return call(
        ffn_forward_kernel,
        "ffn_forward",
        [shape((2 * share, units), bf16)] * 2 + [shape((share, model), bf16)] * 2,
        (xa, xb, up, bias, down),
        scratch=[pltpu.VMEM((2 * share, model), f32)],
        us=4,
    )


def ffn_backward_kernel(ga_ref, gb_ref, up_ref, down_ref, slope_ref, gh_ref, pa_ref, pb_ref, sum_ref, acc_ref):
    share, units = ga_ref.shape[0], up_ref.shape[1]
    tile = min(TILE, units)
    grads = jnp.concatenate([ga_ref[...], gb_ref[...]], 0)
    sum_ref[...] = jnp.zeros_like(sum_ref)
    for j in range(units // tile):
        cols = slice(j * tile, (j + 1) * tile)
        gh = (nt(grads, down_ref[cols, :]) * slope_ref[:, cols].astype(f32)).astype(bf16)
        gh_ref[:, cols] = gh
        sum_ref[0:1, cols] = column_sum(gh.astype(f32))
        part = nt(gh, up_ref[:, cols])
        if j == 0:
            acc_ref[...] = part
        else:
            acc_ref[...] += part
    pa_ref[...] = acc_ref[:share, :].astype(bf16)
    pb_ref[...] = acc_ref[share:, :].astype(bf16)


def ffn_backward(ga, gb, up, down, slope):
    share, model = ga.shape
    units = up.shape[1]
    return call(
        ffn_backward_kernel,
        "ffn_backward",
        [shape((2 * share, units), bf16)] + [shape((share, model), bf16)] * 2 + [shape((8, units), f32)],
        (ga, gb, up, down, slope),
        scratch=[pltpu.VMEM((2 * share, model), f32)],
        us=3.3,
    )


def row_blocks(refs, count):
    each = count // len(refs)
    size = refs[0].shape[0] // each
    return [ref.at[s * size : (s + 1) * size, :] for ref in refs for s in range(each)]


def weight_grad_kernel(n_left, n_right, place, *refs):
    lefts, rights, rest = refs[:n_left], refs[n_left : n_left + n_right], refs[n_left + n_right :]
    count = max(n_left, n_right)
    lefts, rights = row_blocks(lefts, count), row_blocks(rights, count)
    rows = lefts[0].shape[1]
    tile = min(TILE, rows)
    for j in range(rows // tile):
        total = None
        for left, right in zip(lefts, rights):
            part = tn(left[:, j * tile : (j + 1) * tile], right[...])
            total = part if total is None else total + part
        place(j, total.astype(bf16), *rest)


def weight_grad(lefts, rights, name):
    rows, cols = lefts[0].shape[1], rights[0].shape[1]

    def place(j, value, out_ref):
        out_ref[j * value.shape[0] : (j + 1) * value.shape[0], :] = value

    return call(
        functools.partial(weight_grad_kernel, len(lefts), len(rights), place),
        name,
        shape((rows, cols), bf16),
        (*lefts, *rights),
        us=3,
    )


def ffn_weight_grads(actives, grads, normed, hiddens, n_batch):
    model = grads[0].shape[1]
    size = model // n_batch
    n = len(actives)

    def kernel(*refs):
        out_ref = refs[-1]

        def place(side):
            def put(j, value, _):
                for i in range(value.shape[0] // size):
                    out_ref[j * (value.shape[0] // size) + i, side] = value[i * size : (i + 1) * size, :]

            return put

        weight_grad_kernel(n, 2 * n, place(0), *refs[: 3 * n], out_ref)
        weight_grad_kernel(2 * n, n, place(1), *refs[3 * n : 6 * n], out_ref)

    return call(
        kernel,
        "ffn_weight_grads",
        shape((n_batch, 2, size, model), bf16),
        (*actives, *grads, *normed, *hiddens),
        us=6,
        vmem=12,
    )


def grads_final(g, gathered, ffn_rows, out_rows, qkv_rows, tokens):
    n_batch, rows, model = gathered.shape
    chips = n_batch // 2
    width = n_batch * qkv_rows // 3

    def kernel(g_ref, in_ref, down_ref, up_ref, out_ref, q_ref, k_ref, v_ref, *refs):
        row_refs, (query_b_ref, value_b_ref, mean_ref, share_ref, all_ref) = refs[:8], refs[8:]
        small = None
        shared = lax.broadcasted_iota(jnp.int32, (SMALL, 1), 0) != 8
        for b in range(n_batch):
            p, core = divmod(b, 2)
            at = 0
            for ref in (down_ref, up_ref):
                ref[b * ffn_rows : (b + 1) * ffn_rows, :] = in_ref[b, at : at + ffn_rows].astype(f32)
                at += ffn_rows
            start = (core * chips + p) * qkv_rows
            all_ref[start : start + qkv_rows, :] = in_ref[b, at : at + qkv_rows]
            at += qkv_rows
            out_ref[b * out_rows : (b + 1) * out_rows, :] = in_ref[b, at : at + out_rows].astype(f32)
            at += out_rows
            value = in_ref[b, at : at + SMALL].astype(f32) + in_ref[b, at + SMALL : at + 2 * SMALL].astype(f32)
            value = jnp.where(shared | (g_ref[0] == core), value, 0.0)
            small = value if small is None else small + value
        for i, ref in enumerate((q_ref, k_ref, v_ref)):
            ref[...] = jnp.transpose(all_ref[i * width : (i + 1) * width, :].astype(f32))
        for ref, at in zip(row_refs, (0, 1, 2, 3, 5, 6, 7, 8)):
            ref[...] = small[at : at + 1, :]
        query_b_ref[...] = small[9:10, :width]
        value_b_ref[...] = small[10:11, :width]
        count = small[4:5, 1:2]
        mean_ref[...] = small[4:5, 0:1] / count
        share_ref[...] = count / tokens

    flat = [(1, model)] * 8 + [(1, width)] * 2 + [(1, 1)] * 2
    return call(
        kernel,
        "grads_final",
        [shape((n_batch * ffn_rows, model), f32)] * 2
        + [shape((n_batch * out_rows, model), f32)]
        + [shape((model, width), f32)] * 3
        + [shape(dims, f32) for dims in flat],
        (g, gathered),
        scalars=1,
        far=True,
        scratch=[pltpu.VMEM((3 * width, model), bf16)],
    )


def out_grad(c, low, pieces, chips):
    model = low.shape[1]
    width, n_head = pieces[0].shape[1], len(pieces)
    rows = width // (2 * chips)

    def kernel(c_ref, low_ref, *refs):
        ins, (keep_ref, send_ref, all_ref) = refs[:n_head], refs[n_head:]
        c_now = c_ref[0]
        for k, piece in enumerate(ins):
            all_ref[...] = tn(piece[...], low_ref[...]).astype(bf16)
            for j in range(chips):
                to = slice((k * chips + j) * rows, (k * chips + j + 1) * rows)
                for ref, core in ((keep_ref, c_now), (send_ref, 1 - c_now)):
                    ref[to, :] = all_ref[pl.ds(pl.multiple_of((2 * j + core) * rows, rows), rows), :]

    return call(
        kernel,
        "out_weight_grad",
        [shape((n_head * chips * rows, model), bf16)] * 2,
        (c, low, *pieces),
        scalars=1,
        scratch=[pltpu.VMEM((width, model), bf16)],
        us=1,
    )


def fold(p, keep, got, blocks, order):
    chips = len(order)
    rows, cols = keep.shape
    size = rows // (blocks * chips)

    def kernel(p_ref, keep_ref, got_ref, first_ref, second_ref):
        for i, k in enumerate(order):
            out, place = (first_ref, i) if i < chips // 2 else (second_ref, i - chips // 2)
            for j in range(blocks):
                at = rows_at(j * chips + (p_ref[0] ^ k), size)
                total = keep_ref[at, :].astype(f32) + got_ref[at, :].astype(f32)
                to = (place * blocks + j) * size
                out[to : to + size, :] = total.astype(bf16)

    return call(
        kernel,
        "fold_cores",
        [shape((rows // 2, cols), bf16)] * 2,
        (p, keep, got),
        scalars=1,
        us=0.7,
    )


def fold_direct(p, keep, got, chips):
    rows, cols = keep.shape
    size = rows // chips

    def kernel(p_ref, keep_ref, got_ref, *outs):
        for k, out in enumerate(outs):
            at = rows_at(p_ref[0] ^ k, size)
            out[...] = (keep_ref[at, :].astype(f32) + got_ref[at, :].astype(f32)).astype(bf16)

    return call(
        kernel, "fold_cores", [shape((size, cols), bf16)] * chips, (p, keep, got), scalars=1, us=0.7
    )


def build(n_batch, n_head):
    half = n_head // 2
    chips = n_batch // 2
    n_all = n_batch * n_head
    CORE = n_head
    CHIP = 2 * n_head

    def permute(value, mask, among=lambda i: True):
        return lax.ppermute(value, ALL, [(i, i ^ mask) for i in range(n_all) if among(i)])

    def after(value, *earlier):
        return lax.optimization_barrier((value, *earlier))[0]

    def is_native(i):
        return ((i // half) % 2) == ((i // n_head) % 2)

    def is_foreign(i):
        return not is_native(i)

    def rows_of(value, start, count):
        return lax.dynamic_slice_in_dim(value, start, count, 0)

    def exchange_slices(piece):
        return jnp.stack([piece] + [permute(piece, k) for k in range(1, n_head)])

    def bits(count):
        return [1 << i for i in reversed(range(count.bit_length() - 1))]

    def halve(value, masks):
        for mask in masks:
            mid = value.shape[0] // 2
            value = sum_of([value[:mid], permute(value[mid:], mask)])
        return value

    def sum_of(values):
        return sum(v.astype(f32) for v in values).astype(bf16)

    def group_stage(own, work, filler=None, far_first=False):
        fars = [permute(own, dl) for dl in range(1, half)]
        pairs = [(own, permute(own, CORE))]
        last, filled, fars_out, fars_extra = own, None, [], []
        if not far_first:
            extra, near, other = work(0, *pairs[0])
            crossed, last = permute(other, CORE), near
        for dl in range(1, half):
            far = after(fars[dl - 1], last)
            pairs.append((far, permute(far, CORE)))
            far_extra, mine, other = work(dl, *pairs[dl])
            fars_extra.append(far_extra)
            other = permute(other, CORE)
            if filler and dl == half - 1:
                filled = filler(pairs, [extra] + fars_extra)
                other = after(other, filled)
            last = sum_of([mine, other])
            fars_out.append(permute(last, dl))
        if far_first:
            extra, near, other = work(0, after(own, last), pairs[0][1])
            crossed = permute(other, CORE)
            near, *fars_out = lax.optimization_barrier((near, *fars_out))
        return [extra] + fars_extra, pairs, [near, crossed] + fars_out, last, filled

    def on_device(
        inputs, segment_ids, query_weight, query_bias, key_weight, value_weight, value_bias, output_weight,
        output_bias, attn_gain, attn_shift, up_weight, up_bias, down_weight, down_bias, ffn_gain, ffn_shift,
        lexical_weight, out_cotangent, lexical_cotangent,
    ):
        length, model = inputs.shape
        share = out_cotangent.shape[0]
        width = query_weight.shape[1]
        units = up_weight.shape[1]
        pairs = width // LANES
        p, c, g, l = (lax.axis_index(a) for a in ALL)
        h = g * half + l
        b = p * 2 + c
        native = c == g
        scalar = lambda *values: jnp.stack([jnp.asarray(v, jnp.int32) for v in values])
        h_arr, c_arr, p_arr, where_arr = scalar(h), scalar(c), scalar(p), scalar(p, c)
        flags = scalar(native, p)
        row = lambda v: v.reshape(1, -1)
        seg_row = row(segment_ids)

        with jax.named_scope("fetch_weights"):
            up_size, down_size = model // chips, units // chips
            out_piece = width // n_batch
            joint = units == model and out_piece % 16 == 0 and chips == 4 and half == 2
            firsts = [rows_of(up_weight, p * up_size, up_size), rows_of(down_weight, p * down_size, down_size)]
            if joint:
                high = lax.reduce_precision(up_bias, 8, 7)
                middle = lax.reduce_precision(up_bias - high, 8, 7)
                rows = jnp.stack([high, middle, up_bias - high - middle]).astype(bf16)
                firsts = [jnp.concatenate(firsts + [jnp.pad(rows, ((0, SMALL - 3), (0, 0)))], 0)]
            out_sent = after(rows_of(output_weight, b * out_piece, out_piece), *firsts)
            firsts = [permute(x, half, is_native) for x in firsts]
            out_parts = exchange_slices(out_sent)
            out_all = lax.all_gather(out_parts, PLANE, axis=0)
            if not joint:
                out_all = jnp.swapaxes(out_all, 0, 1).reshape(n_head, width, model)

        with jax.named_scope("attention"):
            *heads, mixed_own = (
                lambda q, k, v, m, lt, *pieces: (q, k, v, m, lt, list(pieces))
            )(
                *attn_forward(
                    h_arr, segment_ids, inputs, query_weight, key_weight, value_weight, row(query_bias),
                    row(value_bias), seg_row, n_head,
                )
            )
            mixed_first = mixed_own[0]
            mixed_own = [mixed_own[0]] + [permute(mixed_own[m], m) for m in range(1, n_head)]

        with jax.named_scope("fetch_weights"):
            fetched = []
            for x in firsts:
                x = after(x, mixed_first)
                got = [x] + [permute(x, CHIP * k, is_foreign) for k in range(1, min(chips, 3))]
                x = after(x, *mixed_own)
                fetched.append(got + [permute(x, CHIP * k, is_foreign) for k in range(3, chips)])

        with jax.named_scope("attention_out"):
            normed, normed_low, unit_one, inv_one = attn_out(
                rows_of(inputs, h * share, share),
                out_all,
                [row(output_bias), row(attn_gain), row(attn_shift)],
                mixed_own,
            )

        with jax.named_scope("ffn"):
            if joint:
                up_use, down_use, bias_use = assemble(flags, [up_weight, down_weight], fetched[0], "assemble", up_bias)
            else:
                bias_use = row(jnp.where(native, up_bias, permute(up_bias, half)))
                up_use, down_use = (
                    assemble(flags, [w], got, "assemble")[0] for w, got in zip((up_weight, down_weight), fetched)
                )

            def forward_work(dl, xa, xb):
                active, slope, pa, pb = ffn_forward(xa, xb, up_use, bias_use, down_use)
                return (active, slope), pa, pb

            extras, normed_all, ffn_parts, _, _ = group_stage(normed_low, forward_work, far_first=True)
            actives, slopes = [e[0] for e in extras], [e[1] for e in extras]

        with jax.named_scope("loss"):
            result, lexical, grad_pre_two, grad_two_low, sums_two = loss(
                h_arr,
                normed,
                out_cotangent,
                row(lexical_cotangent.astype(f32)),
                seg_row,
                [row(down_bias), row(ffn_gain), row(ffn_shift), row(lexical_weight)],
                ffn_parts,
            )

        flat = lambda values: [x for pair in values for x in pair]
        with jax.named_scope("ffn_back"):

            def backward_work(dl, ga, gb):
                grad_hidden, pa, pb, sums = ffn_backward(ga, gb, up_use, down_use, slopes[dl])
                return (grad_hidden, sums), pa, pb

            extras, grad_two_all, normed_parts, last, _ = group_stage(grad_two_low, backward_work)
            grad_hiddens = [e[0] for e in extras]
            up_b = sum(e[1][:1] for e in extras)

        with jax.named_scope("ffn_weight_grads"):
            grad_hiddens[-1] = after(grad_hiddens[-1], last)
            if joint:
                both = ffn_weight_grads(actives, flat(grad_two_all), flat(normed_all), grad_hiddens, n_batch)
                both, *normed_parts = lax.optimization_barrier((both, *normed_parts))
                both = both.reshape(2 * model, model)
                ffn_part = lax.psum_scatter(both, "p", scatter_dimension=0, tiled=True)

        with jax.named_scope("attention_out_back"):
            grad_pre_one, grad_one_low, small, *grad_mixed = norm_one_back(
                grad_pre_two, unit_one, inv_one, row(attn_gain), out_all, sums_two, up_b, normed_parts, n_head, width
            )
            grad_mixed = [grad_mixed[0]] + [permute(grad_mixed[m], m) for m in range(1, n_head)]

        q, k, v, m, log_total = heads
        scores_grad = lambda grads: attn_backward(
            scalar(h, c), segment_ids, q, k, v, m, log_total, seg_row, grads, inputs,
            (query_weight, key_weight, value_weight),
        )

        def deliver(part):
            mid = part.shape[0] // 2
            this, that = rows_of(part, c * mid, mid), rows_of(part, (1 - c) * mid, mid)
            return this, permute(that, CORE, is_native), permute(this, half, is_foreign), permute(that, half | CORE, is_foreign)

        def delivered(this, beside, straight, crossed):
            return sum_of([jnp.where(native, this, beside), jnp.where(native, straight, crossed)])

        hold = lax.optimization_barrier
        if joint:
            with jax.named_scope("out_weight_grad"):
                out_keep, out_send = out_grad(c_arr, grad_one_low, mixed_own, chips)
                first, second = fold(p_arr, out_keep, permute(out_send, CORE), n_head, range(chips))
                out_got, *grad_mixed = hold((permute(second, CHIP * 2), *grad_mixed))
                out_sum = sum_of([first, out_got])
                n = out_sum.shape[0] // 2
                grad_mixed[0], out_sum = hold((grad_mixed[0], out_sum))
                out_got = permute(out_sum[n:], CHIP)
            with jax.named_scope("attention_back"):
                bias_sums, in_keep, in_send, keep, send = scores_grad(grad_mixed)
                out_got, in_keep, in_send, keep, send = hold((out_got, in_keep, in_send, keep, send))
            with jax.named_scope("out_weight_grad"):
                out_sum = sum_of([out_sum[:n], out_got]).reshape(n_head, out_piece, model)
                line = [permute(jnp.concatenate([out_sum[i], small], 0), i) for i in range(1, n_head)]
            with jax.named_scope("qkv_weight_grad"):
                ffn_part, *line = hold((ffn_part, *line))
                mid = ffn_part.shape[0] // 2
                this, that = rows_of(ffn_part, c * mid, mid), rows_of(ffn_part, (1 - c) * mid, mid)
                core_got = permute(jnp.concatenate([send, that], 0), CORE)
                beside = core_got[send.shape[0] :]
            with jax.named_scope("ffn_weight_grads"):
                straight = permute(after(this, core_got), half, is_foreign)
                crossed = permute(after(that, core_got), half | CORE, is_foreign)
            with jax.named_scope("qkv_weight_grad"):
                folded = fold_direct(p_arr, keep, core_got, chips)
                folded = [folded[0]] + [permute(folded[k], CHIP * k) for k in range(1, chips)]
                straight, crossed, *folded = hold((straight, crossed, *folded))
                piece = sum_of(folded)
            with jax.named_scope("ffn_weight_grads"):
                ffn_sum = delivered(this, beside, straight, crossed)
            with jax.named_scope("small_grads"):
                out_sum = sum_of([out_sum[0]] + [x[:out_piece] for x in line])
                own, one, two, three = (x.astype(f32) for x in [small] + [x[out_piece:] for x in line])
                pack = jnp.concatenate(
                    [((own + two) + (one + three))[:8], (own + two)[8:9], bias_sums[: SMALL - 9]], 0
                )
            with jax.named_scope("gather_grads"):
                high = lax.reduce_precision(pack, 8, 7)
                sent = [ffn_sum, piece, out_sum, high.astype(bf16), (pack - high).astype(bf16)]
                sent = jnp.concatenate(sent, 0)
                gathered = lax.all_gather(sent, PLANE, axis=0)
                in_got = permute(after(in_send, sent), 1)
                grad_down_w, grad_up_w, grad_out_w, grad_query_w, grad_key_w, grad_value_w, *rest = grads_final(
                    scalar(g), gathered, model // n_batch, out_piece, piece.shape[0], length * n_batch
                )
                down_b, ffn_g, ffn_s, lex_w, out_b, attn_g, attn_s, up_b = (x.reshape(-1) for x in rest[:8])
                query_b, value_b, mean_lexical, active_share = (x.reshape(-1) for x in rest[8:])
                mean_lexical, active_share = mean_lexical.reshape(()), active_share.reshape(())
        else:
            with jax.named_scope("attention_back"):
                bias_sums, in_keep, in_send, keep, send = scores_grad(grad_mixed)
                in_got = permute(in_send, 1)
            with jax.named_scope("weight_grads"):
                parts = [
                    weight_grad(actives, flat(grad_two_all), "down_weight_grad"),
                    weight_grad(flat(normed_all), grad_hiddens, "up_weight_grad"),
                ]
                parts = [lax.psum_scatter(x, "p", scatter_dimension=0, tiled=True) for x in parts]
                grad_down_w, grad_up_w = (
                    lax.all_gather(delivered(*deliver(x)), PLANE, axis=0, tiled=True).astype(f32) for x in parts
                )
                parts = [tn(x, grad_one_low).astype(bf16) for x in mixed_own]
                out_sum = sum_of([parts[0]] + [permute(parts[m], m) for m in range(1, n_head)])
                grad_out_w = lax.psum(out_sum, PLANE).astype(f32)
                both = jnp.where(c == 0, jnp.concatenate([keep, send], 0), jnp.concatenate([send, keep], 0))
                grad_query_w, grad_key_w, grad_value_w = jnp.split(lax.psum(both, PLANE).astype(f32).T, 3, 1)
            with jax.named_scope("small_grads"):
                pack = small.astype(f32)
                up_b = lax.psum(pack[8], ("p", "g"))
                up_b = jnp.where(native, up_b, permute(up_b, CORE))[:units]
                pack, biases = lax.psum(pack[:8], ALL), lax.psum(bias_sums, PLANE)
                down_b, ffn_g, ffn_s, lex_w, scalars, out_b, attn_g, attn_s = pack
                query_b, value_b = biases[0, :width], biases[1, :width]
                mean_lexical, active_share = scalars[0] / scalars[1], scalars[1] / (length * n_batch)

        with jax.named_scope("input_grad"):
            parts = sum_of([in_keep, in_got])
            bit = 2
            while bit < half:
                parts = halve(parts, [bit])
                bit *= 2
            mid = parts.shape[0] // 2
            far = permute(parts[mid:], half)
            grad_inputs = (grad_pre_one + parts[:mid].astype(f32) + far.astype(f32)).astype(bf16)

        return (
            result,
            lexical[0],
            grad_inputs,
            grad_query_w,
            query_b,
            grad_key_w,
            grad_value_w,
            value_b,
            grad_out_w,
            out_b,
            attn_g,
            attn_s,
            grad_up_w,
            up_b,
            grad_down_w,
            down_b,
            ffn_g,
            ffn_s,
            lex_w,
            mean_lexical,
            active_share,
        )

    return on_device


def solution(mesh):
    n_batch, n_head = mesh.shape["batch"], mesh.shape["head"]
    fine = Mesh(mesh.devices.reshape(n_batch // 2, 2, 2, n_head // 2), ALL)
    line, tokens = P(LINE), P(ALL)
    rows, columns, whole = P(LINE, None), P(None, LINE), P()
    return jax.shard_map(
        build(n_batch, n_head),
        mesh=fine,
        in_specs=(
            P(PLANE, None), P(PLANE), columns, line, columns, columns, line, rows, whole, whole, whole, columns, line,
            rows, whole, whole, whole, whole, P(ALL, None), tokens,
        ),
        out_specs=(
            P(ALL, None), tokens, P(ALL, None), columns, line, columns, columns, line, rows, whole, whole, whole,
            columns, line, rows, whole, whole, whole, whole, whole, whole,
        ),
        check_vma=False,
    )
```

```python
import functools
import math

import jax
import jax.numpy as jnp
from jax import lax
from jax.experimental import pallas as pl
from jax.experimental.pallas import tpu as pltpu
from jax.sharding import Mesh, PartitionSpec as P

HEAD_DIM = 64
LANES = 128
TILE = 256
SMALL = 16
NORM_EPS = 1e-05
MASKED = -1000000000.0
ALL = ("p", "c", "g", "l")
PLANE = ("p", "c")
LINE = ("g", "l")
f32 = jnp.float32
bf16 = jnp.bfloat16
MIB = 2**20
VMEM = pl.BlockSpec(memory_space=pltpu.VMEM)
SMEM = pl.BlockSpec(memory_space=pltpu.SMEM)
HBM = pl.BlockSpec(memory_space=pltpu.HBM)


def shape(dims, dtype):
    return jax.ShapeDtypeStruct(dims, dtype)


def nn(left, right):
    return jnp.dot(left, right, preferred_element_type=f32)


def nt(left, right):
    return lax.dot_general(left, right, (((1,), (1,)), ((), ())), preferred_element_type=f32)


def tn(left, right):
    return lax.dot_general(left, right, (((0,), (0,)), ((), ())), preferred_element_type=f32)


def call(kernel, name, out_shape, args, scalars=0, scratch=(), us=1.0, vmem=12, far=False, cols=None):
    many = isinstance(out_shape, (list, tuple))
    outs = list(out_shape) if many else [out_shape]
    n_in, n_out = len(args), len(outs)
    far_in = range(scalars, n_in) if far else ()
    far_out = range(n_out) if far else ()
    cols = cols or {}
    held = [pltpu.VMEM(args[i].shape[:-1] + ((LANES,) if i in cols else args[i].shape[-1:]), args[i].dtype) for i in far_in]
    held += [pltpu.VMEM(outs[i].shape, outs[i].dtype) for i in far_out]
    n_held = len(held)

    def whole(*refs):
        given, extra = refs[: n_in + n_out], refs[n_in + n_out :]
        use = list(given)
        own, rest = extra[:n_held], extra[n_held:]
        if n_held:
            rest, sems = rest[:-1], rest[-1]
        copies = []
        for slot, i in enumerate(far_in):
            source = given[i]
            if i in cols:
                source = source.at[:, cols[i]]
            copies.append(pltpu.make_async_copy(source, own[slot], sems.at[slot]))
            use[i] = own[slot]
        for copy in copies:
            copy.start()
        for copy in copies:
            copy.wait()
        for slot, i in enumerate(far_out, len(far_in)):
            use[n_in + i] = own[slot]
        kernel(*use, *rest)
        copies = [
            pltpu.make_async_copy(own[slot], given[n_in + i], sems.at[slot]) for slot, i in enumerate(far_out, len(far_in))
        ]
        for copy in copies:
            copy.start()
        for copy in copies:
            copy.wait()

    place = HBM if far else VMEM
    result = pl.pallas_call(
        whole if n_held else kernel,
        out_shape=outs,
        in_specs=[SMEM] * scalars + [place] * (n_in - scalars),
        out_specs=[place] * n_out,
        scratch_shapes=held + list(scratch) + ([pltpu.SemaphoreType.DMA((n_held,))] if n_held else []),
        compiler_params=pltpu.CompilerParams(vmem_limit_bytes=(58 if far else vmem) * MIB),
        cost_estimate=pl.CostEstimate(flops=int(us * 1.1e7), bytes_accessed=int(us * 3.6e4), transcendentals=0),
        name=name,
    )(*args)
    return list(result) if many else result[0]


def rows_at(index, count):
    return pl.ds(pl.multiple_of(index * count, count), count)


def seg_columns(seg_ref, col_ref):
    seg = seg_ref[...].astype(f32)
    col_ref[...] = jnp.transpose(jnp.broadcast_to(seg, (LANES, seg.shape[1])))
    return seg


def key_window(seg_ref, seg_smem, i, block, run):
    length = seg_ref.shape[1]
    first = seg_smem[i * block].astype(f32)
    last = seg_smem[i * block + block - 1].astype(f32)
    seg = seg_ref[...]
    begin = jnp.sum(jnp.where(seg < first, 1.0, 0.0)).astype(jnp.int32) // LANES
    end = (jnp.sum(jnp.where(seg <= last, 1.0, 0.0)).astype(jnp.int32) + LANES - 1) // LANES
    need = (end - begin) * LANES
    smaller = 0
    for size in (length // 2, 3 * length // 4, length):

        @pl.when((need > smaller) & (need <= size))
        def _(size=size):
            start = jnp.minimum(begin, (length - size) // LANES)
            run(pl.multiple_of(start * LANES, LANES), size)

        smaller = size


def attn_forward_kernel(
    n_head, block, h_ref, segs_ref, x_ref, wq_ref, wk_ref, wv_ref, bq_ref, bv_ref, seg_ref, q_ref, k_ref, v_ref, m_ref,
    lt_ref, *refs
):
    pieces, (col_ref, row_ref) = refs[:n_head], refs[n_head:]
    length, width = q_ref.shape
    share = length // n_head
    x = x_ref[...]
    q_ref[...] = ((nn(x, wq_ref[...]) + bq_ref[...]) * 0.125).astype(bf16)
    k_ref[...] = nn(x, wk_ref[...]).astype(bf16)
    v_ref[...] = (nn(x, wv_ref[...]) + bv_ref[...]).astype(bf16)
    first = lax.broadcasted_iota(jnp.int32, (1, LANES), 1) < HEAD_DIM
    row_ref[...] = seg_columns(seg_ref, col_ref)

    def step(i, _):
        rows = rows_at(i, block)

        def run(start, size):
            keys = pl.ds(start, size)
            same = col_ref[rows, 0:1] == row_ref[:, keys]
            for pair in range(width // LANES):
                cols = slice(pair * LANES, (pair + 1) * LANES)
                q, k, v = q_ref[rows, cols], k_ref[keys, cols], v_ref[keys, cols]
                outs, tops = [], []
                for odd in range(2):
                    mine = jnp.logical_not(first) if odd else first
                    scores = jnp.where(same, nt(jnp.where(mine, q, jnp.zeros_like(q)), k), MASKED)
                    top = jnp.max(scores, -1, keepdims=True)
                    probs = jnp.exp(scores - top).astype(bf16)
                    outs.append(nn(probs, jnp.where(mine, v, jnp.ones_like(v))))
                    tops.append(top)
                total = jnp.where(first, outs[1], outs[0])
                mix = jnp.where(first, outs[0], outs[1]) / pltpu.roll(total, HEAD_DIM, 1)
                m_ref[rows, cols] = mix.astype(bf16)
                lt_ref[rows, cols] = jnp.where(first, tops[1], tops[0]) + jnp.log(total)

        key_window(row_ref, segs_ref, i, block, run)
        return 0

    lax.fori_loop(0, length // block, step, 0)
    h = h_ref[0]
    for k, piece in enumerate(pieces):
        piece[...] = m_ref[rows_at(h ^ k, share), :]


def attn_forward(h, segs, x, wq, wk, wv, bq, bv, seg_row, n_head, block=256):
    length, model = x.shape
    width = wq.shape[1]
    return call(
        functools.partial(attn_forward_kernel, n_head, block),
        "attention_forward",
        [shape((length, width), bf16)] * 4
        + [shape((length, width), f32)]
        + [shape((length // n_head, width), bf16)] * n_head,
        (h, segs, x, wq, wk, wv, bq, bv, seg_row),
        scalars=2,
        far=True,
        scratch=[pltpu.VMEM((length, LANES), f32), pltpu.VMEM((1, length), f32)],
        us=12,
    )


def attn_backward_kernel(n_head, block, where_ref, segs_ref, q_ref, k_ref, v_ref, m_ref, lt_ref, seg_ref, *refs):
    g_pieces, refs = refs[:n_head], refs[n_head:]
    x_ref, weights, bias_ref, in_keep_ref, in_send_ref, keep_ref, send_ref = refs[0], refs[1:4], *refs[4:9]
    g_ref, row_ref, col_ref, seg_row_ref, gk_ref, gv_ref, out_ref, all_ref = refs[9:]
    h_ref = where_ref
    length, width = q_ref.shape
    share = length // n_head
    h = h_ref[0]
    for k, piece in enumerate(g_pieces):
        g_ref[rows_at(h ^ k, share), :] = piece[...]
    first = lax.broadcasted_iota(jnp.int32, (1, LANES), 1) < HEAD_DIM
    seg_row_ref[...] = seg_columns(seg_ref, col_ref)
    row_ref[0:width, :] = jnp.transpose(lt_ref[...])
    prod = g_ref[...].astype(f32) * m_ref[...].astype(f32)
    head = lax.broadcasted_iota(jnp.int32, (8, width), 0)
    col = lax.broadcasted_iota(jnp.int32, (8, width), 1)
    pick = jnp.where(col // HEAD_DIM == head, 1.0, 0.0).astype(bf16)
    high = prod.astype(bf16)
    low = (prod - high.astype(f32)).astype(bf16)
    row_ref[width : width + 8, :] = nt(pick, high) + nt(pick, low)
    gk_ref[...] = jnp.zeros_like(gk_ref)
    gv_ref[...] = jnp.zeros_like(gv_ref)

    def step(i, _):
        rows = rows_at(i, block)

        def run(start, size):
            keys = pl.ds(start, size)
            same = col_ref[keys, 0:1] == seg_row_ref[:, rows]
            for pair in range(width // LANES):
                cols = slice(pair * LANES, (pair + 1) * LANES)
                q, k, v, g = q_ref[rows, cols], k_ref[keys, cols], v_ref[keys, cols], g_ref[rows, cols]
                gq, gk, gv = jnp.zeros((block, LANES), f32), gk_ref[keys, cols], gv_ref[keys, cols]
                for odd in range(2):
                    mine = jnp.logical_not(first) if odd else first
                    place = pair * LANES + (0 if odd else HEAD_DIM)
                    log_total = row_ref[place : place + 1, rows]
                    inner = row_ref[width + 2 * pair + odd : width + 2 * pair + odd + 1, rows]
                    q_mine, g_mine = jnp.where(mine, q, jnp.zeros_like(q)), jnp.where(mine, g, jnp.zeros_like(g))
                    probs = jnp.exp(jnp.where(same, nt(k, q_mine), MASKED) - log_total)
                    gv = gv + nn(probs.astype(bf16), g_mine)
                    gs = (probs * (nt(v, g_mine) - inner)).astype(bf16)
                    gk = gk + nn(gs, q_mine)
                    gq = gq + tn(gs, jnp.where(mine, k, jnp.zeros_like(k)))
                gk_ref[keys, cols], gv_ref[keys, cols] = gk, gv
                out_ref[rows, cols] = gq.astype(bf16) * bf16(0.125)

        key_window(seg_row_ref, segs_ref, i, block, run)
        return 0

    lax.fori_loop(0, length // block, step, 0)
    out_ref[:, width : 2 * width] = gk_ref[...].astype(bf16)
    out_ref[:, 2 * width :] = gv_ref[...].astype(bf16)
    bias_ref[...] = jnp.zeros_like(bias_ref)
    bias_ref[0:1, 0:width] = column_sum(out_ref[:, :width].astype(f32))
    bias_ref[1:2, 0:width] = column_sum(out_ref[:, 2 * width :].astype(f32))
    for place, k in enumerate(halves_order(n_head)):
        rows = rows_at(h ^ k, share)
        total = None
        for i, weight in enumerate(weights):
            part = nt(out_ref[rows, i * width : (i + 1) * width], weight[...])
            total = part if total is None else total + part
        side, at = divmod(place, n_head // 2)
        (in_keep_ref, in_send_ref)[side][at * share : (at + 1) * share, :] = total.astype(bf16)
    tile = min(TILE, 3 * width)
    for j in range(3 * width // tile):
        at = slice(j * tile, (j + 1) * tile)
        all_ref[at, :] = tn(out_ref[:, at], x_ref[...]).astype(bf16)
    mid = 3 * width // 2
    keep_ref[...] = all_ref[rows_at(where_ref[1], mid), :]
    send_ref[...] = all_ref[rows_at(1 - where_ref[1], mid), :]


def halves_order(count):
    if count == 1:
        return [0]
    evens = [2 * i for i in halves_order(count // 2)]
    return evens + [i + 1 for i in evens]


def attn_backward(where, segs, q, k, v, m, log_total, seg_row, grads, x, weights, block=256):
    length, width = q.shape
    model = x.shape[1]
    n_head = len(grads)
    return call(
        functools.partial(attn_backward_kernel, n_head, block),
        "attention_backward",
        [shape((8, model), f32)]
        + [shape((length // 2, model), bf16)] * 2
        + [shape((3 * width // 2, model), bf16)] * 2,
        (where, segs, q, k, v, m, log_total, seg_row, *grads, x, *weights),
        scalars=2,
        far=True,
        scratch=[
            pltpu.VMEM((length, width), bf16),
            pltpu.VMEM((width + 8, length), f32),
            pltpu.VMEM((length, LANES), f32),
            pltpu.VMEM((1, length), f32),
            pltpu.VMEM((length, width), f32),
            pltpu.VMEM((length, width), f32),
            pltpu.VMEM((length, 3 * width), bf16),
            pltpu.VMEM((3 * width, model), bf16),
        ],
        us=18,
    )


def mean(value):
    return jnp.mean(value, -1, keepdims=True)


def norm_back(grad, unit, inv, gain):
    gg = grad * gain
    return inv * (gg - mean(gg) - unit * mean(gg * unit))


def column_sum(value):
    return jnp.sum(value, 0, keepdims=True)


def slice_of(ref, k):
    if len(ref.shape) == 3:
        return ref[k]
    return jnp.concatenate([ref[i, k] for i in range(ref.shape[0])], 0)


def attn_out_kernel(n_head, x_ref, w_ref, bias_ref, gain_ref, shift_ref, *refs):
    pieces, (normed_ref, low_ref, unit_ref, inv_ref) = refs[:n_head], refs[n_head:]
    total = None
    for k, piece in enumerate(pieces):
        part = nn(piece[...], slice_of(w_ref, k)).astype(bf16).astype(f32)
        total = part if total is None else total + part
    pre = x_ref[...].astype(f32) + total + bias_ref[...]
    center = pre - mean(pre)
    inv = lax.rsqrt(mean(center * center) + NORM_EPS)
    unit = center * inv
    normed = unit * gain_ref[...] + shift_ref[...]
    normed_ref[...] = normed
    low_ref[...] = normed.astype(bf16)
    unit_ref[...] = unit
    inv_ref[...] = jnp.broadcast_to(inv, inv_ref.shape)


def attn_out(x_own, weight, vectors, pieces):
    share, model = x_own.shape
    return call(
        functools.partial(attn_out_kernel, len(pieces)),
        "attention_out_norm",
        [
            shape((share, model), f32),
            shape((share, model), bf16),
            shape((share, model), f32),
            shape((share, LANES), f32),
        ],
        (x_own, weight, *vectors, *pieces),
        us=1.5,
    )


def loss_kernel(h_ref, normed_ref, cot_ref, lexcot_ref, seg_ref, *refs):
    (down_b_ref, gain_ref, shift_ref, lexw_ref), refs = refs[:4], refs[4:]
    parts, (result_ref, lex_ref, grad_ref, low_ref, sums_ref, later_ref) = refs[:-6], refs[-6:]
    share, model = normed_ref.shape
    total = parts[0][...].astype(f32)
    for part in parts[1:]:
        total = total + part[...].astype(f32)
    pre = normed_ref[...] + total + down_b_ref[...]
    gain, lex_w = gain_ref[...], lexw_ref[...]
    center = pre - mean(pre)
    inv = lax.rsqrt(mean(center * center) + NORM_EPS)
    unit = center * inv
    final = unit * gain + shift_ref[...]
    result_ref[...] = final.astype(bf16)
    lex_cot = jnp.transpose(jnp.broadcast_to(lexcot_ref[...], (LANES, share)))[:, 0:1]
    lex_in = jnp.sum(final * lex_w, -1, keepdims=True)
    away = jnp.exp(-jnp.abs(lex_in))
    scale = lex_cot * (jnp.where(lex_in >= 0, 1.0, away) / (1.0 + away))
    lexical = jnp.maximum(lex_in, 0.0) + jnp.log1p(away)
    lex_row = jnp.transpose(jnp.broadcast_to(lexical, (share, LANES)))[0:8, :]
    lex_ref[...] = lex_row
    grad_final = cot_ref[...].astype(f32) + scale * lex_w
    grad = norm_back(grad_final, unit, inv, gain)
    grad_ref[...] = grad
    low_ref[...] = grad.astype(bf16)
    seg = jnp.broadcast_to(seg_ref[...].astype(f32), later_ref.shape)
    place = lax.broadcasted_iota(jnp.int32, later_ref.shape, 1)
    later_ref[...] = jnp.where((seg == pltpu.roll(seg, 1, 1)) & (place > 0), 1.0, 0.0)
    later = later_ref[0:1, rows_at(h_ref[0], share)]
    lane = lax.broadcasted_iota(jnp.int32, (1, model), 1)
    lex_sum = jnp.sum(lex_row[0:1, :] * later, -1, keepdims=True)
    count = jnp.sum(later, -1, keepdims=True)
    sums_ref[...] = jnp.zeros_like(sums_ref)
    sums_ref[0:1, :] = column_sum(grad)
    sums_ref[1:2, :] = column_sum(grad_final * unit)
    sums_ref[2:3, :] = column_sum(grad_final)
    sums_ref[3:4, :] = column_sum(scale * final)
    sums_ref[4:5, :] = jnp.where(lane == 0, lex_sum, 0.0) + jnp.where(lane == 1, count, 0.0)


def loss(h, normed, cotangent, lex_cot, seg_row, vectors, parts):
    share, model = normed.shape
    return call(
        loss_kernel,
        "loss_norm_back",
        [
            shape((share, model), bf16),
            shape((8, share), f32),
            shape((share, model), f32),
            shape((share, model), bf16),
            shape((8, model), f32),
        ],
        (h, normed, cotangent, lex_cot, seg_row, *vectors, *parts),
        scalars=1,
        scratch=[pltpu.VMEM((8, seg_row.shape[1]), f32)],
        us=2.5,
    )


def norm_one_back_kernel(n_head, grad_ref, unit_ref, inv_ref, gain_ref, w_ref, sums_two_ref, up_ref, *refs):
    n_out = 3 + n_head
    parts, outs = refs[: -n_out - 1], refs[-n_out - 1 : -1]
    pre_ref, low_ref, parts_ref = outs[:3]
    small_ref = refs[-1]
    grad = grad_ref[...]
    for part in parts:
        grad = grad + part[...].astype(f32)
    unit = unit_ref[...]
    pre = norm_back(grad, unit, inv_ref[:, 0:1], gain_ref[0:1, :])
    pre_ref[...] = pre
    low = pre.astype(bf16)
    low_ref[...] = low
    for k in range(n_head):
        outs[3 + k][...] = nt(low, slice_of(w_ref, k)).astype(bf16)
    small_ref[...] = jnp.zeros_like(small_ref)
    small_ref[0:5, :] = sums_two_ref[0:5, :]
    small_ref[5:6, :] = column_sum(pre)
    small_ref[6:7, :] = column_sum(grad * unit)
    small_ref[7:8, :] = column_sum(grad)
    small_ref[8:9, 0 : up_ref.shape[1]] = up_ref[...]
    parts_ref[...] = small_ref[...].astype(bf16)


def norm_one_back(grad, unit, inv, gain, weight, sums_two, up_sums, parts, n_head, width):
    share, model = grad.shape
    return call(
        functools.partial(norm_one_back_kernel, n_head),
        "norm_one_back",
        [shape((share, model), f32), shape((share, model), bf16), shape((SMALL, model), bf16)]
        + [shape((share, width), bf16)] * n_head,
        (grad, unit, inv, gain, weight, sums_two, up_sums, *parts),
        far=True,
        scratch=[pltpu.VMEM((SMALL, model), f32)],
        us=1.5,
    )


def assemble(flags, natives, pieces, name, bias=None):
    n_in, n_pieces = len(natives), len(pieces)
    args = [*natives, *pieces] + ([bias.reshape(1, -1)] if bias is not None else [])

    def kernel(flag_ref, *refs):
        own, parts, outs = refs[:n_in], refs[n_in : n_in + n_pieces], refs[len(args) : -2]
        tail_ref, sems = refs[-2:]

        def run(copies):
            for copy in copies:
                copy.start()
            for copy in copies:
                copy.wait()

        @pl.when(flag_ref[0] == 1)
        def _():
            run([pltpu.make_async_copy(own[i], outs[i], sems.at[i]) for i in range(n_in)])
            if bias is not None:
                outs[n_in][...] = refs[len(args) - 1][...]

        @pl.when(flag_ref[0] == 0)
        def _():
            copies, offset = [], 0
            for out_ref in outs[:n_in]:
                rows = out_ref.shape[0] // n_pieces
                for k, piece in enumerate(parts):
                    source = piece.at[offset : offset + rows, :]
                    target = out_ref.at[rows_at(flag_ref[1] ^ k, rows), :]
                    copies.append(pltpu.make_async_copy(source, target, sems.at[len(copies)]))
                offset += rows
            if bias is not None:
                copies.append(pltpu.make_async_copy(parts[0].at[offset : offset + SMALL, :], tail_ref, sems.at[len(copies)]))
            run(copies)
            if bias is not None:
                rows = tail_ref[...].astype(f32)
                outs[n_in][...] = rows[0:1] + rows[1:2] + rows[2:3]

    out_shape = [shape(native.shape, bf16) for native in natives]
    out_shape += [shape((1, bias.shape[0]), f32)] if bias is not None else []
    return list(
        pl.pallas_call(
            kernel,
            out_shape=out_shape,
            in_specs=[SMEM] + [HBM] * (n_in + n_pieces) + ([VMEM] if bias is not None else []),
            out_specs=[VMEM] * len(out_shape),
            scratch_shapes=[
                pltpu.VMEM((SMALL, pieces[0].shape[1]), bf16),
                pltpu.SemaphoreType.DMA((n_in * n_pieces + 1,)),
            ],
            compiler_params=pltpu.CompilerParams(vmem_limit_bytes=12 * MIB),
            cost_estimate=pl.CostEstimate(flops=1000, bytes_accessed=100000, transcendentals=0),
            name=name,
        )(flags, *args)
    )


def ffn_forward_kernel(xa_ref, xb_ref, up_ref, bias_ref, down_ref, act_ref, slope_ref, pa_ref, pb_ref, acc_ref):
    share, units = xa_ref.shape[0], up_ref.shape[1]
    tile = min(TILE, units)
    x = jnp.concatenate([xa_ref[...], xb_ref[...]], 0)
    for j in range(units // tile):
        cols = slice(j * tile, (j + 1) * tile)
        hidden = nn(x, up_ref[:, cols]) + bias_ref[:, cols]
        below = 0.5 * (1.0 + lax.erf(hidden * math.sqrt(0.5)))
        active = (hidden * below).astype(bf16)
        act_ref[:, cols] = active
        slope_ref[:, cols] = (
            below + hidden * (jnp.exp(-0.5 * hidden * hidden) * (1.0 / math.sqrt(2 * math.pi)))
        ).astype(bf16)
        part = nn(active, down_ref[cols, :])
        if j == 0:
            acc_ref[...] = part
        else:
            acc_ref[...] += part
    pa_ref[...] = acc_ref[:share, :].astype(bf16)
    pb_ref[...] = acc_ref[share:, :].astype(bf16)


def ffn_forward(xa, xb, up, bias, down):
    share, model = xa.shape
    units = up.shape[1]
    return call(
        ffn_forward_kernel,
        "ffn_forward",
        [shape((2 * share, units), bf16)] * 2 + [shape((share, model), bf16)] * 2,
        (xa, xb, up, bias, down),
        scratch=[pltpu.VMEM((2 * share, model), f32)],
        us=4,
    )


def ffn_backward_kernel(ga_ref, gb_ref, up_ref, down_ref, slope_ref, gh_ref, pa_ref, pb_ref, sum_ref, acc_ref):
    share, units = ga_ref.shape[0], up_ref.shape[1]
    tile = min(TILE, units)
    grads = jnp.concatenate([ga_ref[...], gb_ref[...]], 0)
    sum_ref[...] = jnp.zeros_like(sum_ref)
    for j in range(units // tile):
        cols = slice(j * tile, (j + 1) * tile)
        gh = (nt(grads, down_ref[cols, :]) * slope_ref[:, cols].astype(f32)).astype(bf16)
        gh_ref[:, cols] = gh
        sum_ref[0:1, cols] = column_sum(gh.astype(f32))
        part = nt(gh, up_ref[:, cols])
        if j == 0:
            acc_ref[...] = part
        else:
            acc_ref[...] += part
    pa_ref[...] = acc_ref[:share, :].astype(bf16)
    pb_ref[...] = acc_ref[share:, :].astype(bf16)


def ffn_backward(ga, gb, up, down, slope):
    share, model = ga.shape
    units = up.shape[1]
    return call(
        ffn_backward_kernel,
        "ffn_backward",
        [shape((2 * share, units), bf16)] + [shape((share, model), bf16)] * 2 + [shape((8, units), f32)],
        (ga, gb, up, down, slope),
        scratch=[pltpu.VMEM((2 * share, model), f32)],
        us=3.3,
    )


def row_blocks(refs, count):
    each = count // len(refs)
    size = refs[0].shape[0] // each
    return [ref.at[s * size : (s + 1) * size, :] for ref in refs for s in range(each)]


def weight_grad_kernel(n_left, n_right, place, *refs):
    lefts, rights, rest = refs[:n_left], refs[n_left : n_left + n_right], refs[n_left + n_right :]
    count = max(n_left, n_right)
    lefts, rights = row_blocks(lefts, count), row_blocks(rights, count)
    rows = lefts[0].shape[1]
    tile = min(TILE, rows)
    for j in range(rows // tile):
        total = None
        for left, right in zip(lefts, rights):
            part = tn(left[:, j * tile : (j + 1) * tile], right[...])
            total = part if total is None else total + part
        place(j, total.astype(bf16), *rest)


def weight_grad(lefts, rights, name):
    rows, cols = lefts[0].shape[1], rights[0].shape[1]

    def place(j, value, out_ref):
        out_ref[j * value.shape[0] : (j + 1) * value.shape[0], :] = value

    return call(
        functools.partial(weight_grad_kernel, len(lefts), len(rights), place),
        name,
        shape((rows, cols), bf16),
        (*lefts, *rights),
        us=3,
    )


def ffn_weight_grads(actives, grads, normed, hiddens, n_batch):
    model = grads[0].shape[1]
    size = model // n_batch
    n = len(actives)

    def kernel(*refs):
        out_ref = refs[-1]

        def place(side):
            def put(j, value, _):
                for i in range(value.shape[0] // size):
                    out_ref[j * (value.shape[0] // size) + i, side] = value[i * size : (i + 1) * size, :]

            return put

        weight_grad_kernel(n, 2 * n, place(0), *refs[: 3 * n], out_ref)
        weight_grad_kernel(2 * n, n, place(1), *refs[3 * n : 6 * n], out_ref)

    return call(
        kernel,
        "ffn_weight_grads",
        shape((n_batch, 2, size, model), bf16),
        (*actives, *grads, *normed, *hiddens),
        us=6,
        vmem=12,
    )


def grads_final(g, gathered, ffn_rows, out_rows, qkv_rows, tokens):
    n_batch, rows, model = gathered.shape
    chips = n_batch // 2
    width = n_batch * qkv_rows // 3
    flat = [(1, model)] * 8 + [(1, width)] * 2 + [(1, 1)] * 2
    big = [(n_batch * ffn_rows, model)] * 2 + [(n_batch * out_rows, model)] + [(model, width)] * 3

    def kernel(g_ref, in_ref, *refs):
        big_refs, flat_refs = refs[: len(big)], refs[len(big) : len(big) + len(flat)]
        held_ref, all_ref, *wide, in_sems, out_sems = refs[len(big) + len(flat) :]
        arrive = [pltpu.make_async_copy(in_ref.at[b], held_ref.at[b], in_sems.at[b]) for b in range(n_batch)]
        for copy in arrive:
            copy.start()
        leave, small = [], None

        def send(source, target):
            leave.append(pltpu.make_async_copy(source, target, out_sems.at[len(leave)]))
            leave[-1].start()

        shared = lax.broadcasted_iota(jnp.int32, (SMALL, 1), 0) != 8
        for b in range(n_batch):
            p, core = divmod(b, 2)
            arrive[b].wait()
            at = 0
            for i, size in enumerate((ffn_rows, ffn_rows)):
                to = slice(b * size, (b + 1) * size)
                wide[i][to, :] = held_ref[b, at : at + size].astype(f32)
                send(wide[i].at[to, :], big_refs[i].at[to, :])
                at += size
            start = (core * chips + p) * qkv_rows
            all_ref[start : start + qkv_rows, :] = held_ref[b, at : at + qkv_rows]
            at += qkv_rows
            wide[2][b * out_rows : (b + 1) * out_rows, :] = held_ref[b, at : at + out_rows].astype(f32)
            at += out_rows
            value = held_ref[b, at : at + SMALL].astype(f32) + held_ref[b, at + SMALL : at + 2 * SMALL].astype(f32)
            value = jnp.where(shared | (g_ref[0] == core), value, 0.0)
            small = value if small is None else small + value
        send(wide[2], big_refs[2])
        for i in range(3):
            wide[3 + i][...] = jnp.transpose(all_ref[i * width : (i + 1) * width, :].astype(f32))
            send(wide[3 + i], big_refs[3 + i])
        for ref, at in zip(flat_refs, (0, 1, 2, 3, 5, 6, 7, 8)):
            ref[...] = small[at : at + 1, :]
        query_b_ref, value_b_ref, mean_ref, share_ref = flat_refs[8:]
        query_b_ref[...] = small[9:10, :width]
        value_b_ref[...] = small[10:11, :width]
        count = small[4:5, 1:2]
        mean_ref[...] = small[4:5, 0:1] / count
        share_ref[...] = count / tokens
        for copy in leave:
            copy.wait()

    return list(
        pl.pallas_call(
            kernel,
            out_shape=[shape(dims, f32) for dims in big + flat],
            in_specs=[SMEM, HBM],
            out_specs=[HBM] * len(big) + [VMEM] * len(flat),
            scratch_shapes=[pltpu.VMEM(gathered.shape, bf16), pltpu.VMEM((3 * width, model), bf16)]
            + [pltpu.VMEM(dims, f32) for dims in big]
            + [pltpu.SemaphoreType.DMA((n_batch,)), pltpu.SemaphoreType.DMA((2 * n_batch + 4,))],
            compiler_params=pltpu.CompilerParams(vmem_limit_bytes=58 * MIB),
            cost_estimate=pl.CostEstimate(flops=1000, bytes_accessed=100000, transcendentals=0),
            name="grads_final",
        )(g, gathered)
    )


def out_grad(c, low, pieces, chips):
    model = low.shape[1]
    width, n_head = pieces[0].shape[1], len(pieces)
    rows = width // (2 * chips)

    def kernel(c_ref, low_ref, *refs):
        ins, (keep_ref, send_ref, all_ref) = refs[:n_head], refs[n_head:]
        c_now = c_ref[0]
        for k, piece in enumerate(ins):
            all_ref[...] = tn(piece[...], low_ref[...]).astype(bf16)
            for j in range(chips):
                to = slice((k * chips + j) * rows, (k * chips + j + 1) * rows)
                for ref, core in ((keep_ref, c_now), (send_ref, 1 - c_now)):
                    ref[to, :] = all_ref[pl.ds(pl.multiple_of((2 * j + core) * rows, rows), rows), :]

    return call(
        kernel,
        "out_weight_grad",
        [shape((n_head * chips * rows, model), bf16)] * 2,
        (c, low, *pieces),
        scalars=1,
        scratch=[pltpu.VMEM((width, model), bf16)],
        us=1,
    )


def fold_direct(p, keep, got, chips, blocks=1):
    rows, cols = keep.shape
    size = rows // (blocks * chips)

    def kernel(p_ref, keep_ref, got_ref, *outs):
        for k, out in enumerate(outs):
            for j in range(blocks):
                at = rows_at(j * chips + (p_ref[0] ^ k), size)
                total = keep_ref[at, :].astype(f32) + got_ref[at, :].astype(f32)
                out[j * size : (j + 1) * size, :] = total.astype(bf16)

    return call(
        kernel, "fold_cores", [shape((blocks * size, cols), bf16)] * chips, (p, keep, got), scalars=1, us=0.7
    )


def build(n_batch, n_head):
    half = n_head // 2
    chips = n_batch // 2
    n_all = n_batch * n_head
    CORE = n_head
    CHIP = 2 * n_head

    def permute(value, mask, among=lambda i: True):
        return lax.ppermute(value, ALL, [(i, i ^ mask) for i in range(n_all) if among(i)])

    def after(value, *earlier):
        return lax.optimization_barrier((value, *earlier))[0]

    def is_native(i):
        return ((i // half) % 2) == ((i // n_head) % 2)

    def is_foreign(i):
        return not is_native(i)

    def rows_of(value, start, count):
        return lax.dynamic_slice_in_dim(value, start, count, 0)

    def exchange_slices(piece):
        return jnp.stack([piece] + [permute(piece, k) for k in range(1, n_head)])

    def bits(count):
        return [1 << i for i in reversed(range(count.bit_length() - 1))]

    def halve(value, masks):
        for mask in masks:
            mid = value.shape[0] // 2
            value = sum_of([value[:mid], permute(value[mid:], mask)])
        return value

    def sum_of(values):
        return sum(v.astype(f32) for v in values).astype(bf16)

    def group_stage(own, work, filler=None, far_first=False):
        fars = [permute(own, dl) for dl in range(1, half)]
        pairs = [(own, permute(own, CORE))]
        last, filled, fars_out, fars_extra = own, None, [], []
        if not far_first:
            extra, near, other = work(0, *pairs[0])
            crossed, last = permute(other, CORE), near
        for dl in range(1, half):
            far = after(fars[dl - 1], last)
            pairs.append((far, permute(far, CORE)))
            far_extra, mine, other = work(dl, *pairs[dl])
            fars_extra.append(far_extra)
            other = permute(other, CORE)
            if filler and dl == half - 1:
                filled = filler(pairs, [extra] + fars_extra)
                other = after(other, filled)
            last = sum_of([mine, other])
            fars_out.append(permute(last, dl))
        if far_first:
            extra, near, other = work(0, after(own, last), pairs[0][1])
            crossed = permute(other, CORE)
            near, *fars_out = lax.optimization_barrier((near, *fars_out))
        return [extra] + fars_extra, pairs, [near, crossed] + fars_out, last, filled

    def on_device(
        inputs, segment_ids, query_weight, query_bias, key_weight, value_weight, value_bias, output_weight,
        output_bias, attn_gain, attn_shift, up_weight, up_bias, down_weight, down_bias, ffn_gain, ffn_shift,
        lexical_weight, out_cotangent, lexical_cotangent,
    ):
        length, model = inputs.shape
        share = out_cotangent.shape[0]
        width = query_weight.shape[1]
        units = up_weight.shape[1]
        pairs = width // LANES
        p, c, g, l = (lax.axis_index(a) for a in ALL)
        h = g * half + l
        b = p * 2 + c
        native = c == g
        scalar = lambda *values: jnp.stack([jnp.asarray(v, jnp.int32) for v in values])
        h_arr, c_arr, p_arr, where_arr = scalar(h), scalar(c), scalar(p), scalar(p, c)
        flags = scalar(native, p)
        row = lambda v: v.reshape(1, -1)
        seg_row = row(segment_ids)

        with jax.named_scope("fetch_weights"):
            up_size, down_size = model // chips, units // chips
            out_piece = width // n_batch
            joint = units == model and out_piece % 16 == 0 and chips == 4 and half == 2
            firsts = [rows_of(up_weight, p * up_size, up_size), rows_of(down_weight, p * down_size, down_size)]
            if joint:
                high = lax.reduce_precision(up_bias, 8, 7)
                middle = lax.reduce_precision(up_bias - high, 8, 7)
                rows = jnp.stack([high, middle, up_bias - high - middle]).astype(bf16)
                firsts = [jnp.concatenate(firsts + [jnp.pad(rows, ((0, SMALL - 3), (0, 0)))], 0)]
            out_sent = after(rows_of(output_weight, b * out_piece, out_piece), *firsts)
            firsts = [permute(x, half, is_native) for x in firsts]
            out_parts = exchange_slices(out_sent)
            out_all = lax.all_gather(out_parts, PLANE, axis=0)
            if not joint:
                out_all = jnp.swapaxes(out_all, 0, 1).reshape(n_head, width, model)

        with jax.named_scope("attention"):
            *heads, mixed_own = (
                lambda q, k, v, m, lt, *pieces: (q, k, v, m, lt, list(pieces))
            )(
                *attn_forward(
                    h_arr, segment_ids, inputs, query_weight, key_weight, value_weight, row(query_bias),
                    row(value_bias), seg_row, n_head,
                )
            )
            mixed_first = mixed_own[0]
            mixed_own = [mixed_own[0]] + [permute(mixed_own[m], m) for m in range(1, n_head)]

        with jax.named_scope("fetch_weights"):
            fetched = []
            for x in firsts:
                x = after(x, mixed_first)
                got = [x] + [permute(x, CHIP * k, is_foreign) for k in range(1, min(chips, 3))]
                x = after(x, *mixed_own)
                fetched.append(got + [permute(x, CHIP * k, is_foreign) for k in range(3, chips)])

        with jax.named_scope("attention_out"):
            normed, normed_low, unit_one, inv_one = attn_out(
                rows_of(inputs, h * share, share),
                out_all,
                [row(output_bias), row(attn_gain), row(attn_shift)],
                mixed_own,
            )

        with jax.named_scope("ffn"):
            if joint:
                up_use, down_use, bias_use = assemble(flags, [up_weight, down_weight], fetched[0], "assemble", up_bias)
            else:
                bias_use = row(jnp.where(native, up_bias, permute(up_bias, half)))
                up_use, down_use = (
                    assemble(flags, [w], got, "assemble")[0] for w, got in zip((up_weight, down_weight), fetched)
                )

            def forward_work(dl, xa, xb):
                active, slope, pa, pb = ffn_forward(xa, xb, up_use, bias_use, down_use)
                return (active, slope), pa, pb

            extras, normed_all, ffn_parts, _, _ = group_stage(normed_low, forward_work, far_first=True)
            actives, slopes = [e[0] for e in extras], [e[1] for e in extras]

        with jax.named_scope("loss"):
            result, lexical, grad_pre_two, grad_two_low, sums_two = loss(
                h_arr,
                normed,
                out_cotangent,
                row(lexical_cotangent.astype(f32)),
                seg_row,
                [row(down_bias), row(ffn_gain), row(ffn_shift), row(lexical_weight)],
                ffn_parts,
            )

        flat = lambda values: [x for pair in values for x in pair]
        with jax.named_scope("ffn_back"):

            def backward_work(dl, ga, gb):
                grad_hidden, pa, pb, sums = ffn_backward(ga, gb, up_use, down_use, slopes[dl])
                return (grad_hidden, sums), pa, pb

            extras, grad_two_all, normed_parts, last, _ = group_stage(grad_two_low, backward_work)
            grad_hiddens = [e[0] for e in extras]
            up_b = sum(e[1][:1] for e in extras)

        with jax.named_scope("ffn_weight_grads"):
            grad_hiddens[-1] = after(grad_hiddens[-1], last)
            if joint:
                both = ffn_weight_grads(actives, flat(grad_two_all), flat(normed_all), grad_hiddens, n_batch)
                both, *normed_parts = lax.optimization_barrier((both, *normed_parts))
                both = both.reshape(2 * model, model)
                ffn_part = lax.psum_scatter(both, "p", scatter_dimension=0, tiled=True)

        with jax.named_scope("attention_out_back"):
            grad_pre_one, grad_one_low, small, *grad_mixed = norm_one_back(
                grad_pre_two, unit_one, inv_one, row(attn_gain), out_all, sums_two, up_b, normed_parts, n_head, width
            )
            grad_mixed = [grad_mixed[0]] + [permute(grad_mixed[m], m) for m in range(1, n_head)]

        q, k, v, m, log_total = heads
        scores_grad = lambda grads: attn_backward(
            scalar(h, c), segment_ids, q, k, v, m, log_total, seg_row, grads, inputs,
            (query_weight, key_weight, value_weight),
        )

        def deliver(part):
            mid = part.shape[0] // 2
            this, that = rows_of(part, c * mid, mid), rows_of(part, (1 - c) * mid, mid)
            return this, permute(that, CORE, is_native), permute(this, half, is_foreign), permute(that, half | CORE, is_foreign)

        def delivered(this, beside, straight, crossed):
            return sum_of([jnp.where(native, this, beside), jnp.where(native, straight, crossed)])

        hold = lax.optimization_barrier
        if joint:
            with jax.named_scope("out_weight_grad"):
                out_keep, out_send = out_grad(c_arr, grad_one_low, mixed_own, chips)
                out_got, *grad_mixed = hold((permute(out_send, CORE), *grad_mixed))
                out_parts = fold_direct(p_arr, out_keep, out_got, chips, n_head)
                grad_mixed[0], out_parts[0] = hold((grad_mixed[0], out_parts[0]))
                out_parts = [out_parts[0]] + [permute(out_parts[i], CHIP * i) for i in range(1, chips)]
            with jax.named_scope("attention_back"):
                bias_sums, in_keep, in_send, keep, send = scores_grad(grad_mixed)
                in_keep, in_send, keep, send, *out_parts = hold((in_keep, in_send, keep, send, *out_parts))
            with jax.named_scope("out_weight_grad"):
                out_sum = sum_of(out_parts).reshape(n_head, out_piece, model)
                line = [permute(jnp.concatenate([out_sum[i], small], 0), i) for i in range(1, n_head)]
            with jax.named_scope("qkv_weight_grad"):
                ffn_part, *line = hold((ffn_part, *line))
                mid = ffn_part.shape[0] // 2
                this, that = rows_of(ffn_part, c * mid, mid), rows_of(ffn_part, (1 - c) * mid, mid)
                core_got = permute(jnp.concatenate([send, that], 0), CORE)
                beside = core_got[send.shape[0] :]
            with jax.named_scope("ffn_weight_grads"):
                straight = permute(after(this, core_got), half, is_foreign)
                crossed = permute(after(that, core_got), half | CORE, is_foreign)
            with jax.named_scope("qkv_weight_grad"):
                folded = fold_direct(p_arr, keep, core_got, chips)
                folded = [folded[0]] + [permute(folded[k], CHIP * k) for k in range(1, chips)]
                straight, crossed, *folded = hold((straight, crossed, *folded))
                piece = sum_of(folded)
            with jax.named_scope("ffn_weight_grads"):
                ffn_sum = delivered(this, beside, straight, crossed)
            with jax.named_scope("small_grads"):
                out_sum = sum_of([out_sum[0]] + [x[:out_piece] for x in line])
                own, one, two, three = (x.astype(f32) for x in [small] + [x[out_piece:] for x in line])
                pack = jnp.concatenate(
                    [((own + two) + (one + three))[:8], (own + two)[8:9], bias_sums[: SMALL - 9]], 0
                )
            with jax.named_scope("gather_grads"):
                high = lax.reduce_precision(pack, 8, 7)
                sent = [ffn_sum, piece, out_sum, high.astype(bf16), (pack - high).astype(bf16)]
                sent = jnp.concatenate(sent, 0)
                gathered = lax.all_gather(sent, PLANE, axis=0)
                in_got = permute(after(in_send, sent), 1)
                grad_down_w, grad_up_w, grad_out_w, grad_query_w, grad_key_w, grad_value_w, *rest = grads_final(
                    scalar(g), gathered, model // n_batch, out_piece, piece.shape[0], length * n_batch
                )
                down_b, ffn_g, ffn_s, lex_w, out_b, attn_g, attn_s, up_b = (x.reshape(-1) for x in rest[:8])
                query_b, value_b, mean_lexical, active_share = (x.reshape(-1) for x in rest[8:])
                mean_lexical, active_share = mean_lexical.reshape(()), active_share.reshape(())
        else:
            with jax.named_scope("attention_back"):
                bias_sums, in_keep, in_send, keep, send = scores_grad(grad_mixed)
                in_got = permute(in_send, 1)
            with jax.named_scope("weight_grads"):
                parts = [
                    weight_grad(actives, flat(grad_two_all), "down_weight_grad"),
                    weight_grad(flat(normed_all), grad_hiddens, "up_weight_grad"),
                ]
                parts = [lax.psum_scatter(x, "p", scatter_dimension=0, tiled=True) for x in parts]
                grad_down_w, grad_up_w = (
                    lax.all_gather(delivered(*deliver(x)), PLANE, axis=0, tiled=True).astype(f32) for x in parts
                )
                parts = [tn(x, grad_one_low).astype(bf16) for x in mixed_own]
                out_sum = sum_of([parts[0]] + [permute(parts[m], m) for m in range(1, n_head)])
                grad_out_w = lax.psum(out_sum, PLANE).astype(f32)
                both = jnp.where(c == 0, jnp.concatenate([keep, send], 0), jnp.concatenate([send, keep], 0))
                grad_query_w, grad_key_w, grad_value_w = jnp.split(lax.psum(both, PLANE).astype(f32).T, 3, 1)
            with jax.named_scope("small_grads"):
                pack = small.astype(f32)
                up_b = lax.psum(pack[8], ("p", "g"))
                up_b = jnp.where(native, up_b, permute(up_b, CORE))[:units]
                pack, biases = lax.psum(pack[:8], ALL), lax.psum(bias_sums, PLANE)
                down_b, ffn_g, ffn_s, lex_w, scalars, out_b, attn_g, attn_s = pack
                query_b, value_b = biases[0, :width], biases[1, :width]
                mean_lexical, active_share = scalars[0] / scalars[1], scalars[1] / (length * n_batch)

        with jax.named_scope("input_grad"):
            parts = sum_of([in_keep, in_got])
            bit = 2
            while bit < half:
                parts = halve(parts, [bit])
                bit *= 2
            mid = parts.shape[0] // 2
            far = permute(parts[mid:], half)
            grad_inputs = (grad_pre_one + parts[:mid].astype(f32) + far.astype(f32)).astype(bf16)

        return (
            result,
            lexical[0],
            grad_inputs,
            grad_query_w,
            query_b,
            grad_key_w,
            grad_value_w,
            value_b,
            grad_out_w,
            out_b,
            attn_g,
            attn_s,
            grad_up_w,
            up_b,
            grad_down_w,
            down_b,
            ffn_g,
            ffn_s,
            lex_w,
            mean_lexical,
            active_share,
        )

    return on_device


def solution(mesh):
    n_batch, n_head = mesh.shape["batch"], mesh.shape["head"]
    fine = Mesh(mesh.devices.reshape(n_batch // 2, 2, 2, n_head // 2), ALL)
    line, tokens = P(LINE), P(ALL)
    rows, columns, whole = P(LINE, None), P(None, LINE), P()
    return jax.shard_map(
        build(n_batch, n_head),
        mesh=fine,
        in_specs=(
            P(PLANE, None), P(PLANE), columns, line, columns, columns, line, rows, whole, whole, whole, columns, line,
            rows, whole, whole, whole, whole, P(ALL, None), tokens,
        ),
        out_specs=(
            P(ALL, None), tokens, P(ALL, None), columns, line, columns, columns, line, rows, whole, whole, whole,
            columns, line, rows, whole, whole, whole, whole, whole, whole,
        ),
        check_vma=False,
    )
```

```python
import functools
import math

import jax
import jax.numpy as jnp
from jax import lax
from jax.experimental import pallas as pl
from jax.experimental.pallas import tpu as pltpu
from jax.sharding import Mesh, PartitionSpec as P

HEAD_DIM = 64
LANES = 128
TILE = 256
SMALL = 16
NORM_EPS = 1e-05
MASKED = -1000000000.0
ALL = ("p", "c", "g", "l")
PLANE = ("p", "c")
LINE = ("g", "l")
f32 = jnp.float32
bf16 = jnp.bfloat16
MIB = 2**20
VMEM = pl.BlockSpec(memory_space=pltpu.VMEM)
SMEM = pl.BlockSpec(memory_space=pltpu.SMEM)
HBM = pl.BlockSpec(memory_space=pltpu.HBM)


def shape(dims, dtype):
    return jax.ShapeDtypeStruct(dims, dtype)


def nn(left, right):
    return jnp.dot(left, right, preferred_element_type=f32)


def nt(left, right):
    return lax.dot_general(left, right, (((1,), (1,)), ((), ())), preferred_element_type=f32)


def tn(left, right):
    return lax.dot_general(left, right, (((0,), (0,)), ((), ())), preferred_element_type=f32)


def call(kernel, name, out_shape, args, scalars=0, scratch=(), us=1.0, vmem=12, far=False, cols=None):
    many = isinstance(out_shape, (list, tuple))
    outs = list(out_shape) if many else [out_shape]
    n_in, n_out = len(args), len(outs)
    far_in = range(scalars, n_in) if far else ()
    far_out = range(n_out) if far else ()
    cols = cols or {}
    held = [pltpu.VMEM(args[i].shape[:-1] + ((LANES,) if i in cols else args[i].shape[-1:]), args[i].dtype) for i in far_in]
    held += [pltpu.VMEM(outs[i].shape, outs[i].dtype) for i in far_out]
    n_held = len(held)

    def whole(*refs):
        given, extra = refs[: n_in + n_out], refs[n_in + n_out :]
        use = list(given)
        own, rest = extra[:n_held], extra[n_held:]
        if n_held:
            rest, sems = rest[:-1], rest[-1]
        copies = []
        for slot, i in enumerate(far_in):
            source = given[i]
            if i in cols:
                source = source.at[:, cols[i]]
            copies.append(pltpu.make_async_copy(source, own[slot], sems.at[slot]))
            use[i] = own[slot]
        for copy in copies:
            copy.start()
        for copy in copies:
            copy.wait()
        for slot, i in enumerate(far_out, len(far_in)):
            use[n_in + i] = own[slot]
        kernel(*use, *rest)
        copies = [
            pltpu.make_async_copy(own[slot], given[n_in + i], sems.at[slot]) for slot, i in enumerate(far_out, len(far_in))
        ]
        for copy in copies:
            copy.start()
        for copy in copies:
            copy.wait()

    place = HBM if far else VMEM
    result = pl.pallas_call(
        whole if n_held else kernel,
        out_shape=outs,
        in_specs=[SMEM] * scalars + [place] * (n_in - scalars),
        out_specs=[place] * n_out,
        scratch_shapes=held + list(scratch) + ([pltpu.SemaphoreType.DMA((n_held,))] if n_held else []),
        compiler_params=pltpu.CompilerParams(vmem_limit_bytes=(58 if far else vmem) * MIB),
        cost_estimate=pl.CostEstimate(flops=int(us * 1.1e7), bytes_accessed=int(us * 3.6e4), transcendentals=0),
        name=name,
    )(*args)
    return list(result) if many else result[0]


def rows_at(index, count):
    return pl.ds(pl.multiple_of(index * count, count), count)


def seg_columns(seg_ref, col_ref):
    seg = seg_ref[...].astype(f32)
    col_ref[...] = jnp.transpose(jnp.broadcast_to(seg, (LANES, seg.shape[1])))
    return seg


def key_window(seg_ref, seg_smem, i, block, run):
    length = seg_ref.shape[1]
    first = seg_smem[i * block].astype(f32)
    last = seg_smem[i * block + block - 1].astype(f32)
    seg = seg_ref[...]
    begin = jnp.sum(jnp.where(seg < first, 1.0, 0.0)).astype(jnp.int32) // LANES
    end = (jnp.sum(jnp.where(seg <= last, 1.0, 0.0)).astype(jnp.int32) + LANES - 1) // LANES
    need = (end - begin) * LANES
    smaller = 0
    for size in [eighths * length // 8 for eighths in (3, 4, 5, 6, 8)]:

        @pl.when((need > smaller) & (need <= size))
        def _(size=size):
            start = jnp.minimum(begin, (length - size) // LANES)
            run(pl.multiple_of(start * LANES, LANES), size)

        smaller = size


def attn_forward_kernel(
    n_head, block, h_ref, segs_ref, x_ref, wq_ref, wk_ref, wv_ref, bq_ref, bv_ref, seg_ref, q_ref, k_ref, v_ref, m_ref,
    lt_ref, *refs
):
    pieces, (x_own_ref, col_ref, row_ref) = refs[:n_head], refs[n_head:]
    length, width = q_ref.shape
    share = length // n_head
    x_own_ref[...] = x_ref[rows_at(h_ref[0], share), :]
    x = x_ref[...]
    q_ref[...] = ((nn(x, wq_ref[...]) + bq_ref[...]) * 0.125).astype(bf16)
    k_ref[...] = nn(x, wk_ref[...]).astype(bf16)
    v_ref[...] = (nn(x, wv_ref[...]) + bv_ref[...]).astype(bf16)
    first = lax.broadcasted_iota(jnp.int32, (1, LANES), 1) < HEAD_DIM
    row_ref[...] = seg_columns(seg_ref, col_ref)

    def step(i, _):
        rows = rows_at(i, block)

        def run(start, size):
            keys = pl.ds(start, size)
            same = col_ref[rows, 0:1] == row_ref[:, keys]
            for pair in range(width // LANES):
                cols = slice(pair * LANES, (pair + 1) * LANES)
                q, k, v = q_ref[rows, cols], k_ref[keys, cols], v_ref[keys, cols]
                outs, tops = [], []
                for odd in range(2):
                    mine = jnp.logical_not(first) if odd else first
                    scores = jnp.where(same, nt(jnp.where(mine, q, jnp.zeros_like(q)), k), MASKED)
                    top = jnp.max(scores, -1, keepdims=True)
                    probs = jnp.exp(scores - top).astype(bf16)
                    outs.append(nn(probs, jnp.where(mine, v, jnp.ones_like(v))))
                    tops.append(top)
                total = jnp.where(first, outs[1], outs[0])
                mix = jnp.where(first, outs[0], outs[1]) / pltpu.roll(total, HEAD_DIM, 1)
                m_ref[rows, cols] = mix.astype(bf16)
                lt_ref[rows, cols] = jnp.where(first, tops[1], tops[0]) + jnp.log(total)

        key_window(row_ref, segs_ref, i, block, run)
        return 0

    lax.fori_loop(0, length // block, step, 0)
    h = h_ref[0]
    for k, piece in enumerate(pieces):
        piece[...] = m_ref[rows_at(h ^ k, share), :]


def attn_forward(h, segs, x, wq, wk, wv, bq, bv, seg_row, n_head, block=256):
    length, model = x.shape
    width = wq.shape[1]
    return call(
        functools.partial(attn_forward_kernel, n_head, block),
        "attention_forward",
        [shape((length, width), bf16)] * 4
        + [shape((length, width), f32)]
        + [shape((length // n_head, width), bf16)] * n_head
        + [shape((length // n_head, model), bf16)],
        (h, segs, x, wq, wk, wv, bq, bv, seg_row),
        scalars=2,
        far=True,
        scratch=[pltpu.VMEM((length, LANES), f32), pltpu.VMEM((1, length), f32)],
        us=12,
    )


def attn_backward_kernel(n_head, block, where_ref, segs_ref, q_ref, k_ref, v_ref, m_ref, lt_ref, seg_ref, *refs):
    g_pieces, refs = refs[:n_head], refs[n_head:]
    x_ref, weights, bias_ref, in_keep_ref, in_send_ref, keep_ref, send_ref = refs[0], refs[1:4], *refs[4:9]
    g_ref, row_ref, col_ref, seg_row_ref, gk_ref, gv_ref, out_ref, all_ref = refs[9:]
    h_ref = where_ref
    length, width = q_ref.shape
    share = length // n_head
    h = h_ref[0]
    for k, piece in enumerate(g_pieces):
        g_ref[rows_at(h ^ k, share), :] = piece[...]
    first = lax.broadcasted_iota(jnp.int32, (1, LANES), 1) < HEAD_DIM
    seg_row_ref[...] = seg_columns(seg_ref, col_ref)
    row_ref[0:width, :] = jnp.transpose(lt_ref[...])
    prod = g_ref[...].astype(f32) * m_ref[...].astype(f32)
    head = lax.broadcasted_iota(jnp.int32, (8, width), 0)
    col = lax.broadcasted_iota(jnp.int32, (8, width), 1)
    pick = jnp.where(col // HEAD_DIM == head, 1.0, 0.0).astype(bf16)
    high = prod.astype(bf16)
    low = (prod - high.astype(f32)).astype(bf16)
    row_ref[width : width + 8, :] = nt(pick, high) + nt(pick, low)
    gk_ref[...] = jnp.zeros_like(gk_ref)
    gv_ref[...] = jnp.zeros_like(gv_ref)

    def step(i, _):
        rows = rows_at(i, block)

        def run(start, size):
            keys = pl.ds(start, size)
            same = col_ref[keys, 0:1] == seg_row_ref[:, rows]
            for pair in range(width // LANES):
                cols = slice(pair * LANES, (pair + 1) * LANES)
                q, k, v, g = q_ref[rows, cols], k_ref[keys, cols], v_ref[keys, cols], g_ref[rows, cols]
                gq, gk, gv = jnp.zeros((block, LANES), f32), gk_ref[keys, cols], gv_ref[keys, cols]
                for odd in range(2):
                    mine = jnp.logical_not(first) if odd else first
                    place = pair * LANES + (0 if odd else HEAD_DIM)
                    log_total = row_ref[place : place + 1, rows]
                    inner = row_ref[width + 2 * pair + odd : width + 2 * pair + odd + 1, rows]
                    q_mine, g_mine = jnp.where(mine, q, jnp.zeros_like(q)), jnp.where(mine, g, jnp.zeros_like(g))
                    probs = jnp.exp(jnp.where(same, nt(k, q_mine), MASKED) - log_total)
                    gv = gv + nn(probs.astype(bf16), g_mine)
                    gs = (probs * (nt(v, g_mine) - inner)).astype(bf16)
                    gk = gk + nn(gs, q_mine)
                    gq = gq + tn(gs, jnp.where(mine, k, jnp.zeros_like(k)))
                gk_ref[keys, cols], gv_ref[keys, cols] = gk, gv
                out_ref[rows, cols] = gq.astype(bf16) * bf16(0.125)

        key_window(seg_row_ref, segs_ref, i, block, run)
        return 0

    lax.fori_loop(0, length // block, step, 0)
    out_ref[:, width : 2 * width] = gk_ref[...].astype(bf16)
    out_ref[:, 2 * width :] = gv_ref[...].astype(bf16)
    bias_ref[...] = jnp.zeros_like(bias_ref)
    bias_ref[0:1, 0:width] = column_sum(out_ref[:, :width].astype(f32))
    bias_ref[1:2, 0:width] = column_sum(out_ref[:, 2 * width :].astype(f32))
    for place, k in enumerate(halves_order(n_head)):
        rows = rows_at(h ^ k, share)
        total = None
        for i, weight in enumerate(weights):
            part = nt(out_ref[rows, i * width : (i + 1) * width], weight[...])
            total = part if total is None else total + part
        side, at = divmod(place, n_head // 2)
        (in_keep_ref, in_send_ref)[side][at * share : (at + 1) * share, :] = total.astype(bf16)
    tile = min(TILE, 3 * width)
    for j in range(3 * width // tile):
        at = slice(j * tile, (j + 1) * tile)
        all_ref[at, :] = tn(out_ref[:, at], x_ref[...]).astype(bf16)
    mid = 3 * width // 2
    keep_ref[...] = all_ref[rows_at(where_ref[1], mid), :]
    send_ref[...] = all_ref[rows_at(1 - where_ref[1], mid), :]


def halves_order(count):
    if count == 1:
        return [0]
    evens = [2 * i for i in halves_order(count // 2)]
    return evens + [i + 1 for i in evens]


def attn_backward(where, segs, q, k, v, m, log_total, seg_row, grads, x, weights, block=256):
    length, width = q.shape
    model = x.shape[1]
    n_head = len(grads)
    return call(
        functools.partial(attn_backward_kernel, n_head, block),
        "attention_backward",
        [shape((8, model), f32)]
        + [shape((length // 2, model), bf16)] * 2
        + [shape((3 * width // 2, model), bf16)] * 2,
        (where, segs, q, k, v, m, log_total, seg_row, *grads, x, *weights),
        scalars=2,
        far=True,
        scratch=[
            pltpu.VMEM((length, width), bf16),
            pltpu.VMEM((width + 8, length), f32),
            pltpu.VMEM((length, LANES), f32),
            pltpu.VMEM((1, length), f32),
            pltpu.VMEM((length, width), f32),
            pltpu.VMEM((length, width), f32),
            pltpu.VMEM((length, 3 * width), bf16),
            pltpu.VMEM((3 * width, model), bf16),
        ],
        us=18,
    )


def mean(value):
    return jnp.mean(value, -1, keepdims=True)


def norm_back(grad, unit, inv, gain):
    gg = grad * gain
    return inv * (gg - mean(gg) - unit * mean(gg * unit))


def column_sum(value):
    return jnp.sum(value, 0, keepdims=True)


def slice_of(ref, k):
    if len(ref.shape) == 3:
        return ref[k]
    return jnp.concatenate([ref[i, k] for i in range(ref.shape[0])], 0)


def attn_out_kernel(n_head, x_ref, w_ref, bias_ref, gain_ref, shift_ref, *refs):
    pieces, (normed_ref, low_ref, unit_ref, inv_ref) = refs[:n_head], refs[n_head:]
    total = None
    for k, piece in enumerate(pieces):
        part = nn(piece[...], slice_of(w_ref, k)).astype(bf16).astype(f32)
        total = part if total is None else total + part
    pre = x_ref[...].astype(f32) + total + bias_ref[...]
    center = pre - mean(pre)
    inv = lax.rsqrt(mean(center * center) + NORM_EPS)
    unit = center * inv
    normed = unit * gain_ref[...] + shift_ref[...]
    normed_ref[...] = normed
    low_ref[...] = normed.astype(bf16)
    unit_ref[...] = unit
    inv_ref[...] = jnp.broadcast_to(inv, inv_ref.shape)


def attn_out(x_own, weight, vectors, pieces):
    share, model = x_own.shape
    return call(
        functools.partial(attn_out_kernel, len(pieces)),
        "attention_out_norm",
        [
            shape((share, model), f32),
            shape((share, model), bf16),
            shape((share, model), f32),
            shape((share, LANES), f32),
        ],
        (x_own, weight, *vectors, *pieces),
        far=True,
        us=1.5,
    )


def loss_kernel(h_ref, normed_ref, cot_ref, lexcot_ref, seg_ref, *refs):
    (down_b_ref, gain_ref, shift_ref, lexw_ref), refs = refs[:4], refs[4:]
    parts, (result_ref, lex_ref, grad_ref, low_ref, sums_ref, later_ref) = refs[:-6], refs[-6:]
    share, model = normed_ref.shape
    total = parts[0][...].astype(f32)
    for part in parts[1:]:
        total = total + part[...].astype(f32)
    pre = normed_ref[...] + total + down_b_ref[...]
    gain, lex_w = gain_ref[...], lexw_ref[...]
    center = pre - mean(pre)
    inv = lax.rsqrt(mean(center * center) + NORM_EPS)
    unit = center * inv
    final = unit * gain + shift_ref[...]
    result_ref[...] = final.astype(bf16)
    lex_cot = jnp.transpose(jnp.broadcast_to(lexcot_ref[...], (LANES, share)))[:, 0:1]
    lex_in = jnp.sum(final * lex_w, -1, keepdims=True)
    away = jnp.exp(-jnp.abs(lex_in))
    scale = lex_cot * (jnp.where(lex_in >= 0, 1.0, away) / (1.0 + away))
    lexical = jnp.maximum(lex_in, 0.0) + jnp.log1p(away)
    lex_row = jnp.transpose(jnp.broadcast_to(lexical, (share, LANES)))[0:8, :]
    lex_ref[...] = lex_row
    grad_final = cot_ref[...].astype(f32) + scale * lex_w
    grad = norm_back(grad_final, unit, inv, gain)
    grad_ref[...] = grad
    low_ref[...] = grad.astype(bf16)
    seg = jnp.broadcast_to(seg_ref[...].astype(f32), later_ref.shape)
    place = lax.broadcasted_iota(jnp.int32, later_ref.shape, 1)
    later_ref[...] = jnp.where((seg == pltpu.roll(seg, 1, 1)) & (place > 0), 1.0, 0.0)
    later = later_ref[0:1, rows_at(h_ref[0], share)]
    lane = lax.broadcasted_iota(jnp.int32, (1, model), 1)
    lex_sum = jnp.sum(lex_row[0:1, :] * later, -1, keepdims=True)
    count = jnp.sum(later, -1, keepdims=True)
    sums_ref[...] = jnp.zeros_like(sums_ref)
    sums_ref[0:1, :] = column_sum(grad)
    sums_ref[1:2, :] = column_sum(grad_final * unit)
    sums_ref[2:3, :] = column_sum(grad_final)
    sums_ref[3:4, :] = column_sum(scale * final)
    sums_ref[4:5, :] = jnp.where(lane == 0, lex_sum, 0.0) + jnp.where(lane == 1, count, 0.0)


def loss(h, normed, cotangent, lex_cot, seg_row, vectors, parts):
    share, model = normed.shape
    return call(
        loss_kernel,
        "loss_norm_back",
        [
            shape((share, model), bf16),
            shape((8, share), f32),
            shape((share, model), f32),
            shape((share, model), bf16),
            shape((8, model), f32),
        ],
        (h, normed, cotangent, lex_cot, seg_row, *vectors, *parts),
        scalars=1,
        scratch=[pltpu.VMEM((8, seg_row.shape[1]), f32)],
        us=2.5,
    )


def norm_one_back_kernel(n_head, grad_ref, unit_ref, inv_ref, gain_ref, w_ref, sums_two_ref, up_ref, *refs):
    n_out = 3 + n_head
    parts, outs = refs[: -n_out - 1], refs[-n_out - 1 : -1]
    pre_ref, low_ref, parts_ref = outs[:3]
    small_ref = refs[-1]
    grad = grad_ref[...]
    for part in parts:
        grad = grad + part[...].astype(f32)
    unit = unit_ref[...]
    pre = norm_back(grad, unit, inv_ref[:, 0:1], gain_ref[0:1, :])
    pre_ref[...] = pre
    low = pre.astype(bf16)
    low_ref[...] = low
    for k in range(n_head):
        outs[3 + k][...] = nt(low, slice_of(w_ref, k)).astype(bf16)
    small_ref[...] = jnp.zeros_like(small_ref)
    small_ref[0:5, :] = sums_two_ref[0:5, :]
    small_ref[5:6, :] = column_sum(pre)
    small_ref[6:7, :] = column_sum(grad * unit)
    small_ref[7:8, :] = column_sum(grad)
    small_ref[8:9, 0 : up_ref.shape[1]] = up_ref[...]
    parts_ref[...] = small_ref[...].astype(bf16)


def norm_one_back(grad, unit, inv, gain, weight, sums_two, up_sums, parts, n_head, width):
    share, model = grad.shape
    return call(
        functools.partial(norm_one_back_kernel, n_head),
        "norm_one_back",
        [shape((share, model), f32), shape((share, model), bf16), shape((SMALL, model), bf16)]
        + [shape((share, width), bf16)] * n_head,
        (grad, unit, inv, gain, weight, sums_two, up_sums, *parts),
        far=True,
        scratch=[pltpu.VMEM((SMALL, model), f32)],
        us=1.5,
    )


def assemble(flags, natives, pieces, name, bias=None):
    n_in, n_pieces = len(natives), len(pieces)
    args = [*natives, *pieces] + ([bias.reshape(1, -1)] if bias is not None else [])

    def kernel(flag_ref, *refs):
        own, parts, outs = refs[:n_in], refs[n_in : n_in + n_pieces], refs[len(args) : -2]
        tail_ref, sems = refs[-2:]

        def run(copies):
            for copy in copies:
                copy.start()
            for copy in copies:
                copy.wait()

        @pl.when(flag_ref[0] == 1)
        def _():
            run([pltpu.make_async_copy(own[i], outs[i], sems.at[i]) for i in range(n_in)])
            if bias is not None:
                outs[n_in][...] = refs[len(args) - 1][...]

        @pl.when(flag_ref[0] == 0)
        def _():
            copies, offset = [], 0
            for out_ref in outs[:n_in]:
                rows = out_ref.shape[0] // n_pieces
                for k, piece in enumerate(parts):
                    source = piece.at[offset : offset + rows, :]
                    target = out_ref.at[rows_at(flag_ref[1] ^ k, rows), :]
                    copies.append(pltpu.make_async_copy(source, target, sems.at[len(copies)]))
                offset += rows
            if bias is not None:
                copies.append(pltpu.make_async_copy(parts[0].at[offset : offset + SMALL, :], tail_ref, sems.at[len(copies)]))
            run(copies)
            if bias is not None:
                rows = tail_ref[...].astype(f32)
                outs[n_in][...] = rows[0:1] + rows[1:2] + rows[2:3]

    out_shape = [shape(native.shape, bf16) for native in natives]
    out_shape += [shape((1, bias.shape[0]), f32)] if bias is not None else []
    return list(
        pl.pallas_call(
            kernel,
            out_shape=out_shape,
            in_specs=[SMEM] + [HBM] * (n_in + n_pieces) + ([VMEM] if bias is not None else []),
            out_specs=[VMEM] * len(out_shape),
            scratch_shapes=[
                pltpu.VMEM((SMALL, pieces[0].shape[1]), bf16),
                pltpu.SemaphoreType.DMA((n_in * n_pieces + 1,)),
            ],
            compiler_params=pltpu.CompilerParams(vmem_limit_bytes=12 * MIB),
            cost_estimate=pl.CostEstimate(flops=1000, bytes_accessed=100000, transcendentals=0),
            name=name,
        )(flags, *args)
    )


def ffn_forward_kernel(xa_ref, xb_ref, up_ref, bias_ref, down_ref, act_ref, slope_ref, pa_ref, pb_ref, acc_ref):
    share, units = xa_ref.shape[0], up_ref.shape[1]
    tile = min(TILE, units)
    x = jnp.concatenate([xa_ref[...], xb_ref[...]], 0)
    for j in range(units // tile):
        cols = slice(j * tile, (j + 1) * tile)
        hidden = nn(x, up_ref[:, cols]) + bias_ref[:, cols]
        below = 0.5 * (1.0 + lax.erf(hidden * math.sqrt(0.5)))
        active = (hidden * below).astype(bf16)
        act_ref[:, cols] = active
        slope_ref[:, cols] = (
            below + hidden * (jnp.exp(-0.5 * hidden * hidden) * (1.0 / math.sqrt(2 * math.pi)))
        ).astype(bf16)
        part = nn(active, down_ref[cols, :])
        if j == 0:
            acc_ref[...] = part
        else:
            acc_ref[...] += part
    pa_ref[...] = acc_ref[:share, :].astype(bf16)
    pb_ref[...] = acc_ref[share:, :].astype(bf16)


def ffn_forward(xa, xb, up, bias, down):
    share, model = xa.shape
    units = up.shape[1]
    return call(
        ffn_forward_kernel,
        "ffn_forward",
        [shape((2 * share, units), bf16)] * 2 + [shape((share, model), bf16)] * 2,
        (xa, xb, up, bias, down),
        scratch=[pltpu.VMEM((2 * share, model), f32)],
        us=4,
    )


def ffn_backward_kernel(ga_ref, gb_ref, up_ref, down_ref, slope_ref, gh_ref, pa_ref, pb_ref, sum_ref, acc_ref):
    share, units = ga_ref.shape[0], up_ref.shape[1]
    tile = min(TILE, units)
    grads = jnp.concatenate([ga_ref[...], gb_ref[...]], 0)
    sum_ref[...] = jnp.zeros_like(sum_ref)
    for j in range(units // tile):
        cols = slice(j * tile, (j + 1) * tile)
        gh = (nt(grads, down_ref[cols, :]) * slope_ref[:, cols].astype(f32)).astype(bf16)
        gh_ref[:, cols] = gh
        sum_ref[0:1, cols] = column_sum(gh.astype(f32))
        part = nt(gh, up_ref[:, cols])
        if j == 0:
            acc_ref[...] = part
        else:
            acc_ref[...] += part
    pa_ref[...] = acc_ref[:share, :].astype(bf16)
    pb_ref[...] = acc_ref[share:, :].astype(bf16)


def ffn_backward(ga, gb, up, down, slope):
    share, model = ga.shape
    units = up.shape[1]
    return call(
        ffn_backward_kernel,
        "ffn_backward",
        [shape((2 * share, units), bf16)] + [shape((share, model), bf16)] * 2 + [shape((8, units), f32)],
        (ga, gb, up, down, slope),
        scratch=[pltpu.VMEM((2 * share, model), f32)],
        us=3.3,
    )


def row_blocks(refs, count):
    each = count // len(refs)
    size = refs[0].shape[0] // each
    return [ref.at[s * size : (s + 1) * size, :] for ref in refs for s in range(each)]


def weight_grad_kernel(n_left, n_right, place, *refs):
    lefts, rights, rest = refs[:n_left], refs[n_left : n_left + n_right], refs[n_left + n_right :]
    count = max(n_left, n_right)
    lefts, rights = row_blocks(lefts, count), row_blocks(rights, count)
    rows = lefts[0].shape[1]
    tile = min(TILE, rows)
    for j in range(rows // tile):
        total = None
        for left, right in zip(lefts, rights):
            part = tn(left[:, j * tile : (j + 1) * tile], right[...])
            total = part if total is None else total + part
        place(j, total.astype(bf16), *rest)


def weight_grad(lefts, rights, name):
    rows, cols = lefts[0].shape[1], rights[0].shape[1]

    def place(j, value, out_ref):
        out_ref[j * value.shape[0] : (j + 1) * value.shape[0], :] = value

    return call(
        functools.partial(weight_grad_kernel, len(lefts), len(rights), place),
        name,
        shape((rows, cols), bf16),
        (*lefts, *rights),
        us=3,
    )


def ffn_weight_grads(actives, grads, normed, hiddens, n_batch):
    model = grads[0].shape[1]
    size = model // n_batch
    n = len(actives)

    def kernel(*refs):
        out_ref = refs[-1]

        def place(side):
            def put(j, value, _):
                for i in range(value.shape[0] // size):
                    out_ref[j * (value.shape[0] // size) + i, side] = value[i * size : (i + 1) * size, :]

            return put

        weight_grad_kernel(n, 2 * n, place(0), *refs[: 3 * n], out_ref)
        weight_grad_kernel(2 * n, n, place(1), *refs[3 * n : 6 * n], out_ref)

    return call(
        kernel,
        "ffn_weight_grads",
        shape((n_batch, 2, size, model), bf16),
        (*actives, *grads, *normed, *hiddens),
        us=6,
        vmem=12,
    )


def grads_final(g, gathered, ffn_rows, out_rows, qkv_rows, tokens):
    n_batch, rows, model = gathered.shape
    chips = n_batch // 2
    width = n_batch * qkv_rows // 3
    flat = [(1, model)] * 8 + [(1, width)] * 2 + [(1, 1)] * 2
    big = [(n_batch * ffn_rows, model)] * 2 + [(n_batch * out_rows, model)] + [(model, width)] * 3

    def kernel(g_ref, in_ref, *refs):
        big_refs, flat_refs = refs[: len(big)], refs[len(big) : len(big) + len(flat)]
        held_ref, all_ref, *wide, in_sems, out_sems = refs[len(big) + len(flat) :]
        arrive = [pltpu.make_async_copy(in_ref.at[b], held_ref.at[b], in_sems.at[b]) for b in range(n_batch)]
        for b in [*range(0, n_batch, 2), *range(1, n_batch, 2)]:
            arrive[b].start()
        leave, small = [], None

        def send(source, target):
            leave.append(pltpu.make_async_copy(source, target, out_sems.at[len(leave)]))
            leave[-1].start()

        shared = lax.broadcasted_iota(jnp.int32, (SMALL, 1), 0) != 8
        done = 0
        for b in [*range(0, n_batch, 2), *range(1, n_batch, 2)]:
            p, core = divmod(b, 2)
            arrive[b].wait()
            at = 0
            for i, size in enumerate((ffn_rows, ffn_rows)):
                to = slice(b * size, (b + 1) * size)
                wide[i][to, :] = held_ref[b, at : at + size].astype(f32)
                send(wide[i].at[to, :], big_refs[i].at[to, :])
                at += size
            start = (core * chips + p) * qkv_rows
            all_ref[start : start + qkv_rows, :] = held_ref[b, at : at + qkv_rows]
            at += qkv_rows
            wide[2][b * out_rows : (b + 1) * out_rows, :] = held_ref[b, at : at + out_rows].astype(f32)
            at += out_rows
            value = held_ref[b, at : at + SMALL].astype(f32) + held_ref[b, at + SMALL : at + 2 * SMALL].astype(f32)
            value = jnp.where(shared | (g_ref[0] == core), value, 0.0)
            small = value if small is None else small + value
            while done < 3 and (done + 1) * width <= start + qkv_rows:
                wide[3 + done][...] = jnp.transpose(all_ref[done * width : (done + 1) * width, :].astype(f32))
                send(wide[3 + done], big_refs[3 + done])
                done += 1
        send(wide[2], big_refs[2])
        for ref, at in zip(flat_refs, (0, 1, 2, 3, 5, 6, 7, 8)):
            ref[...] = small[at : at + 1, :]
        query_b_ref, value_b_ref, mean_ref, share_ref = flat_refs[8:]
        query_b_ref[...] = small[9:10, :width]
        value_b_ref[...] = small[10:11, :width]
        count = small[4:5, 1:2]
        mean_ref[...] = small[4:5, 0:1] / count
        share_ref[...] = count / tokens
        for copy in leave:
            copy.wait()

    return list(
        pl.pallas_call(
            kernel,
            out_shape=[shape(dims, f32) for dims in big + flat],
            in_specs=[SMEM, HBM],
            out_specs=[HBM] * len(big) + [VMEM] * len(flat),
            scratch_shapes=[pltpu.VMEM(gathered.shape, bf16), pltpu.VMEM((3 * width, model), bf16)]
            + [pltpu.VMEM(dims, f32) for dims in big]
            + [pltpu.SemaphoreType.DMA((n_batch,)), pltpu.SemaphoreType.DMA((2 * n_batch + 4,))],
            compiler_params=pltpu.CompilerParams(vmem_limit_bytes=58 * MIB),
            cost_estimate=pl.CostEstimate(flops=1000, bytes_accessed=100000, transcendentals=0),
            name="grads_final",
        )(g, gathered)
    )


def out_grad(c, low, pieces, chips):
    model = low.shape[1]
    width, n_head = pieces[0].shape[1], len(pieces)
    rows = width // (2 * chips)

    def kernel(c_ref, low_ref, *refs):
        ins, (keep_ref, send_ref, all_ref) = refs[:n_head], refs[n_head:]
        c_now = c_ref[0]
        for k, piece in enumerate(ins):
            all_ref[...] = tn(piece[...], low_ref[...]).astype(bf16)
            for j in range(chips):
                to = slice((k * chips + j) * rows, (k * chips + j + 1) * rows)
                for ref, core in ((keep_ref, c_now), (send_ref, 1 - c_now)):
                    ref[to, :] = all_ref[pl.ds(pl.multiple_of((2 * j + core) * rows, rows), rows), :]

    return call(
        kernel,
        "out_weight_grad",
        [shape((n_head * chips * rows, model), bf16)] * 2,
        (c, low, *pieces),
        scalars=1,
        scratch=[pltpu.VMEM((width, model), bf16)],
        us=1,
    )


def fold_direct(p, keep, got, chips, blocks=1):
    rows, cols = keep.shape
    size = rows // (blocks * chips)

    def kernel(p_ref, keep_ref, got_ref, *outs):
        for k, out in enumerate(outs):
            for j in range(blocks):
                at = rows_at(j * chips + (p_ref[0] ^ k), size)
                total = keep_ref[at, :].astype(f32) + got_ref[at, :].astype(f32)
                out[j * size : (j + 1) * size, :] = total.astype(bf16)

    return call(
        kernel, "fold_cores", [shape((blocks * size, cols), bf16)] * chips, (p, keep, got), scalars=1, us=0.7
    )


def build(n_batch, n_head):
    half = n_head // 2
    chips = n_batch // 2
    n_all = n_batch * n_head
    CORE = n_head
    CHIP = 2 * n_head

    def permute(value, mask, among=lambda i: True):
        return lax.ppermute(value, ALL, [(i, i ^ mask) for i in range(n_all) if among(i)])

    def after(value, *earlier):
        return lax.optimization_barrier((value, *earlier))[0]

    def is_native(i):
        return ((i // half) % 2) == ((i // n_head) % 2)

    def is_foreign(i):
        return not is_native(i)

    def rows_of(value, start, count):
        return lax.dynamic_slice_in_dim(value, start, count, 0)

    def exchange_slices(piece):
        return jnp.stack([piece] + [permute(piece, k) for k in range(1, n_head)])

    def bits(count):
        return [1 << i for i in reversed(range(count.bit_length() - 1))]

    def halve(value, masks):
        for mask in masks:
            mid = value.shape[0] // 2
            value = sum_of([value[:mid], permute(value[mid:], mask)])
        return value

    def sum_of(values):
        return sum(v.astype(f32) for v in values).astype(bf16)

    def group_stage(own, work, filler=None, far_first=False):
        fars = [permute(own, dl) for dl in range(1, half)]
        pairs = [(own, permute(own, CORE))]
        last, filled, fars_out, fars_extra = own, None, [], []
        if not far_first:
            extra, near, other = work(0, *pairs[0])
            crossed, last = permute(other, CORE), near
        for dl in range(1, half):
            far = after(fars[dl - 1], last)
            pairs.append((far, permute(far, CORE)))
            far_extra, mine, other = work(dl, *pairs[dl])
            fars_extra.append(far_extra)
            other = permute(other, CORE)
            if filler and dl == half - 1:
                filled = filler(pairs, [extra] + fars_extra)
                other = after(other, filled)
            last = sum_of([mine, other])
            fars_out.append(permute(last, dl))
        if far_first:
            extra, near, other = work(0, after(own, last), pairs[0][1])
            crossed = permute(other, CORE)
            near, *fars_out = lax.optimization_barrier((near, *fars_out))
        return [extra] + fars_extra, pairs, [near, crossed] + fars_out, last, filled

    def on_device(
        inputs, segment_ids, query_weight, query_bias, key_weight, value_weight, value_bias, output_weight,
        output_bias, attn_gain, attn_shift, up_weight, up_bias, down_weight, down_bias, ffn_gain, ffn_shift,
        lexical_weight, out_cotangent, lexical_cotangent,
    ):
        length, model = inputs.shape
        share = out_cotangent.shape[0]
        width = query_weight.shape[1]
        units = up_weight.shape[1]
        pairs = width // LANES
        p, c, g, l = (lax.axis_index(a) for a in ALL)
        h = g * half + l
        b = p * 2 + c
        native = c == g
        scalar = lambda *values: jnp.stack([jnp.asarray(v, jnp.int32) for v in values])
        h_arr, c_arr, p_arr, where_arr = scalar(h), scalar(c), scalar(p), scalar(p, c)
        flags = scalar(native, p)
        row = lambda v: v.reshape(1, -1)
        seg_row = row(segment_ids)

        with jax.named_scope("fetch_weights"):
            up_size, down_size = model // chips, units // chips
            out_piece = width // n_batch
            joint = units == model and out_piece % 16 == 0 and chips == 4 and half == 2
            firsts = [rows_of(up_weight, p * up_size, up_size), rows_of(down_weight, p * down_size, down_size)]
            if joint:
                high = lax.reduce_precision(up_bias, 8, 7)
                middle = lax.reduce_precision(up_bias - high, 8, 7)
                rows = jnp.stack([high, middle, up_bias - high - middle]).astype(bf16)
                firsts[0] = jnp.concatenate([firsts[0], jnp.pad(rows, ((0, SMALL - 3), (0, 0)))], 0)
            out_sent = after(rows_of(output_weight, b * out_piece, out_piece), firsts[0])
            up_first = permute(firsts[0], half, is_native)
            out_parts = exchange_slices(out_sent)
            out_all = lax.all_gather(out_parts, PLANE, axis=0)
            if not joint:
                out_all = jnp.swapaxes(out_all, 0, 1).reshape(n_head, width, model)

        with jax.named_scope("attention"):
            q, k, v, m, log_total, *mixed_own, x_own = attn_forward(
                h_arr, segment_ids, inputs, query_weight, key_weight, value_weight, row(query_bias), row(value_bias),
                seg_row, n_head,
            )
            mixed_first = mixed_own[0]
            mixed_own = [mixed_own[0]] + [permute(mixed_own[i], i) for i in range(1, n_head)]

        with jax.named_scope("fetch_weights"):
            x = after(up_first, mixed_first)
            up_pieces = [x] + [permute(x, CHIP * k, is_foreign) for k in range(1, min(chips, 3))]
            down_first = permute(after(firsts[1], *mixed_own), half, is_native)
            x = after(x, *mixed_own)
            up_pieces += [permute(x, CHIP * k, is_foreign) for k in range(3, chips)]

        with jax.named_scope("attention_out"):
            normed, normed_low, unit_one, inv_one = attn_out(
                x_own,
                out_all,
                [row(output_bias), row(attn_gain), row(attn_shift)],
                mixed_own,
            )

        with jax.named_scope("ffn"):
            x = after(down_first, normed_low, *up_pieces[1 : min(chips, 3)])
            down_pieces = [x] + [permute(x, CHIP * k, is_foreign) for k in range(1, chips)]
            if joint:
                up_use, bias_use = assemble(flags, [up_weight], up_pieces, "assemble_up", up_bias)
            else:
                bias_use = row(jnp.where(native, up_bias, permute(up_bias, half)))
                (up_use,) = assemble(flags, [up_weight], up_pieces, "assemble_up")
            (down_use,) = assemble(flags, [down_weight], down_pieces, "assemble_down")

            def forward_work(dl, xa, xb):
                active, slope, pa, pb = ffn_forward(xa, xb, up_use, bias_use, down_use)
                return (active, slope), pa, pb

            extras, normed_all, ffn_parts, _, _ = group_stage(normed_low, forward_work, far_first=True)
            actives, slopes = [e[0] for e in extras], [e[1] for e in extras]

        with jax.named_scope("loss"):
            result, lexical, grad_pre_two, grad_two_low, sums_two = loss(
                h_arr,
                normed,
                out_cotangent,
                row(lexical_cotangent.astype(f32)),
                seg_row,
                [row(down_bias), row(ffn_gain), row(ffn_shift), row(lexical_weight)],
                ffn_parts,
            )

        flat = lambda values: [x for pair in values for x in pair]
        with jax.named_scope("ffn_back"):

            def backward_work(dl, ga, gb):
                grad_hidden, pa, pb, sums = ffn_backward(ga, gb, up_use, down_use, slopes[dl])
                return (grad_hidden, sums), pa, pb

            extras, grad_two_all, normed_parts, last, _ = group_stage(grad_two_low, backward_work)
            grad_hiddens = [e[0] for e in extras]
            up_b = sum(e[1][:1] for e in extras)

        with jax.named_scope("ffn_weight_grads"):
            grad_hiddens[-1] = after(grad_hiddens[-1], last)
            if joint:
                both = ffn_weight_grads(actives, flat(grad_two_all), flat(normed_all), grad_hiddens, n_batch)
                both, *normed_parts = lax.optimization_barrier((both, *normed_parts))
                both = both.reshape(2 * model, model)
                ffn_part = lax.psum_scatter(both, "p", scatter_dimension=0, tiled=True)

        with jax.named_scope("attention_out_back"):
            grad_pre_one, grad_one_low, small, *grad_mixed = norm_one_back(
                grad_pre_two, unit_one, inv_one, row(attn_gain), out_all, sums_two, up_b, normed_parts, n_head, width
            )
            grad_mixed = [grad_mixed[0]] + [permute(grad_mixed[m], m) for m in range(1, n_head)]

        scores_grad = lambda grads: attn_backward(
            scalar(h, c), segment_ids, q, k, v, m, log_total, seg_row, grads, inputs,
            (query_weight, key_weight, value_weight),
        )

        def deliver(part):
            mid = part.shape[0] // 2
            this, that = rows_of(part, c * mid, mid), rows_of(part, (1 - c) * mid, mid)
            return this, permute(that, CORE, is_native), permute(this, half, is_foreign), permute(that, half | CORE, is_foreign)

        def delivered(this, beside, straight, crossed):
            return sum_of([jnp.where(native, this, beside), jnp.where(native, straight, crossed)])

        hold = lax.optimization_barrier
        if joint:
            with jax.named_scope("out_weight_grad"):
                out_keep, out_send = out_grad(c_arr, grad_one_low, mixed_own, chips)
                out_got, *grad_mixed = hold((permute(out_send, CORE), *grad_mixed))
                out_parts = fold_direct(p_arr, out_keep, out_got, chips, n_head)
                grad_mixed[0], out_parts[0] = hold((grad_mixed[0], out_parts[0]))
                out_parts = [out_parts[0]] + [permute(out_parts[i], CHIP * i) for i in range(1, chips)]
            with jax.named_scope("attention_back"):
                bias_sums, in_keep, in_send, keep, send = scores_grad(grad_mixed)
                in_keep, in_send, keep, send, *out_parts = hold((in_keep, in_send, keep, send, *out_parts))
            with jax.named_scope("out_weight_grad"):
                out_sum = sum_of(out_parts).reshape(n_head, out_piece, model)
                line = [permute(jnp.concatenate([out_sum[i], small], 0), i) for i in range(1, n_head)]
            with jax.named_scope("qkv_weight_grad"):
                ffn_part, *line = hold((ffn_part, *line))
                mid = ffn_part.shape[0] // 2
                this, that = rows_of(ffn_part, c * mid, mid), rows_of(ffn_part, (1 - c) * mid, mid)
                core_got = permute(jnp.concatenate([send, that], 0), CORE)
                beside = core_got[send.shape[0] :]
            with jax.named_scope("ffn_weight_grads"):
                straight = permute(after(this, core_got), half, is_foreign)
                crossed = permute(after(that, core_got), half | CORE, is_foreign)
            with jax.named_scope("qkv_weight_grad"):
                folded = fold_direct(p_arr, keep, core_got, chips)
                folded = [folded[0]] + [permute(folded[k], CHIP * k) for k in range(1, chips)]
                straight, crossed, *folded = hold((straight, crossed, *folded))
                piece = sum_of(folded)
            with jax.named_scope("ffn_weight_grads"):
                ffn_sum = delivered(this, beside, straight, crossed)
            with jax.named_scope("small_grads"):
                out_sum = sum_of([out_sum[0]] + [x[:out_piece] for x in line])
                own, one, two, three = (x.astype(f32) for x in [small] + [x[out_piece:] for x in line])
                pack = jnp.concatenate(
                    [((own + two) + (one + three))[:8], (own + two)[8:9], bias_sums[: SMALL - 9]], 0
                )
            with jax.named_scope("gather_grads"):
                high = lax.reduce_precision(pack, 8, 7)
                sent = [ffn_sum, piece, out_sum, high.astype(bf16), (pack - high).astype(bf16)]
                sent = jnp.concatenate(sent, 0)
                gathered = lax.all_gather(sent, PLANE, axis=0)
                in_got = permute(after(in_send, sent), 1)
                grad_down_w, grad_up_w, grad_out_w, grad_query_w, grad_key_w, grad_value_w, *rest = grads_final(
                    scalar(g), gathered, model // n_batch, out_piece, piece.shape[0], length * n_batch
                )
                down_b, ffn_g, ffn_s, lex_w, out_b, attn_g, attn_s, up_b = (x.reshape(-1) for x in rest[:8])
                query_b, value_b, mean_lexical, active_share = (x.reshape(-1) for x in rest[8:])
                mean_lexical, active_share = mean_lexical.reshape(()), active_share.reshape(())
        else:
            with jax.named_scope("attention_back"):
                bias_sums, in_keep, in_send, keep, send = scores_grad(grad_mixed)
                in_got = permute(in_send, 1)
            with jax.named_scope("weight_grads"):
                parts = [
                    weight_grad(actives, flat(grad_two_all), "down_weight_grad"),
                    weight_grad(flat(normed_all), grad_hiddens, "up_weight_grad"),
                ]
                parts = [lax.psum_scatter(x, "p", scatter_dimension=0, tiled=True) for x in parts]
                grad_down_w, grad_up_w = (
                    lax.all_gather(delivered(*deliver(x)), PLANE, axis=0, tiled=True).astype(f32) for x in parts
                )
                parts = [tn(x, grad_one_low).astype(bf16) for x in mixed_own]
                out_sum = sum_of([parts[0]] + [permute(parts[m], m) for m in range(1, n_head)])
                grad_out_w = lax.psum(out_sum, PLANE).astype(f32)
                both = jnp.where(c == 0, jnp.concatenate([keep, send], 0), jnp.concatenate([send, keep], 0))
                grad_query_w, grad_key_w, grad_value_w = jnp.split(lax.psum(both, PLANE).astype(f32).T, 3, 1)
            with jax.named_scope("small_grads"):
                pack = small.astype(f32)
                up_b = lax.psum(pack[8], ("p", "g"))
                up_b = jnp.where(native, up_b, permute(up_b, CORE))[:units]
                pack, biases = lax.psum(pack[:8], ALL), lax.psum(bias_sums, PLANE)
                down_b, ffn_g, ffn_s, lex_w, scalars, out_b, attn_g, attn_s = pack
                query_b, value_b = biases[0, :width], biases[1, :width]
                mean_lexical, active_share = scalars[0] / scalars[1], scalars[1] / (length * n_batch)

        with jax.named_scope("input_grad"):
            parts = sum_of([in_keep, in_got])
            bit = 2
            while bit < half:
                parts = halve(parts, [bit])
                bit *= 2
            mid = parts.shape[0] // 2
            far = permute(parts[mid:], half)
            grad_inputs = (grad_pre_one + parts[:mid].astype(f32) + far.astype(f32)).astype(bf16)

        return (
            result,
            lexical[0],
            grad_inputs,
            grad_query_w,
            query_b,
            grad_key_w,
            grad_value_w,
            value_b,
            grad_out_w,
            out_b,
            attn_g,
            attn_s,
            grad_up_w,
            up_b,
            grad_down_w,
            down_b,
            ffn_g,
            ffn_s,
            lex_w,
            mean_lexical,
            active_share,
        )

    return on_device


def solution(mesh):
    n_batch, n_head = mesh.shape["batch"], mesh.shape["head"]
    fine = Mesh(mesh.devices.reshape(n_batch // 2, 2, 2, n_head // 2), ALL)
    line, tokens = P(LINE), P(ALL)
    rows, columns, whole = P(LINE, None), P(None, LINE), P()
    return jax.shard_map(
        build(n_batch, n_head),
        mesh=fine,
        in_specs=(
            P(PLANE, None), P(PLANE), columns, line, columns, columns, line, rows, whole, whole, whole, columns, line,
            rows, whole, whole, whole, whole, P(ALL, None), tokens,
        ),
        out_specs=(
            P(ALL, None), tokens, P(ALL, None), columns, line, columns, columns, line, rows, whole, whole, whole,
            columns, line, rows, whole, whole, whole, whole, whole, whole,
        ),
        check_vma=False,
    )
```
